32 devices in a mesh: grp: 2 (over x), pix: 8 (over z, y), disp: 2 (over core).
Axes of the slice: x: 2, y: 2, z: 4, core: 2. Of those that a mesh axis runs over, the one named last changes fastest.
Arguments:
- left_image: int32 [128, 1024], P(('grp', 'pix')), parts along dimension 0, may hold values from 0 to 255
- right_image: int32 [128, 1024], P(('grp', 'pix')), parts along dimension 0, may hold values from 0 to 255
- feat_weight: float32 [16, 16], replicated, may hold values from -1.5 to 1.5
- first_weight: bfloat16 [3, 3, 3, 16, 16], replicated, may hold values from -0.3125 to 0.3125
- first_bias: float32 [16], replicated, may hold values from -3 to 3
- second_weight: bfloat16 [3, 3, 3, 16, 16], replicated, may hold values from -0.3125 to 0.3125
- second_bias: float32 [16], replicated, may hold values from -3 to 3
- head_weight: float32 [16], replicated, may hold values from -1.5 to 1.5
- mask_weight: float32 [16, 144], replicated, may hold values from -1.5 to 1.5
- confidence: float32 [128, 1024], P(('grp', 'pix')), parts along dimension 0, may hold values from 0.1 to 1
Outputs:
- coarse_disparity: float32 [32, 256], P(('grp', 'pix')), parts along dimension 0
- disparity_map: float32 [128, 1024], P(('grp', 'pix')), parts along dimension 0
The draws below stay inside these ranges and needn't reach their ends.
There are 2 independent parts, one for each index of `grp`. The reference program is written for one: setup_inputs(seed, part) draws one part's arguments, and reference() takes and returns one part's arrays. A program takes and returns all parts, laid end to end along the dimension named above; an argument that names none is the same for every part. Nothing has to cross between parts.
All inputs are finite; a program needn't handle non-finite values.
Results may differ from the reference program's by a relative error of at most 0.0065.
Values may be sent and summed in bfloat16 or wider, within the bound.
A program may use at most 64 MiB of HBM per device.

```python
import math
import jax
import jax.numpy as jnp
from jax import lax

CH = 16
DSP = 128
UP = 4
TV_ITERS = 8
FULL_ROWS = 64
FULL_COLS = 1024


def plant(values, stream_key, low, top_value):
    spot = [jax.random.randint(jax.random.fold_in(stream_key, axis), (), 0, length) for axis, length in enumerate(values.shape)]
    widest = values.shape.index(max(values.shape))
    beside = spot[:widest] + [(spot[widest] + 1) % values.shape[widest]] + spot[widest + 1:]
    return values.at[tuple(spot)].set(low).at[tuple(beside)].set(top_value)


def shard_levels(key, extent, shards, low, high):
    loudness = 1.0
    for axis_at, blocks in shards:
        draws = jax.random.uniform(jax.random.fold_in(jax.random.fold_in(key, 6), axis_at), (blocks,), jnp.float32, low / len(shards), high / len(shards))
        loudness = loudness * jnp.repeat(jnp.exp(draws), extent[axis_at] // blocks).reshape((-1,) + (1,) * (len(extent) - 1 - axis_at))
    return loudness


def gaussian(own_key, extent, scale, bound, kind=jnp.bfloat16):
    values = scale * jax.random.normal(own_key, extent, jnp.float32)
    return jnp.clip(values, min=-bound, max=bound).astype(kind)


def setup_inputs(seed: int = 0, part: int = 0) -> dict:
    key_list = jax.random.split(jax.random.key(seed), 11)
    part_splits = jax.random.split(jax.random.fold_in(key_list[10], part), 11)
    return {
        "left_image": plant(jax.random.randint(part_splits[0], (FULL_ROWS, FULL_COLS), 0, 256), jax.random.fold_in(part_splits[0], 1), 0, 255).astype(jnp.int32),
        "right_image": plant(jax.random.randint(part_splits[1], (FULL_ROWS, FULL_COLS), 0, 256), jax.random.fold_in(part_splits[1], 1), 0, 255).astype(jnp.int32),
        "feat_weight": gaussian(key_list[2], (UP * UP, CH), (UP * UP) ** -0.5, 1.5, jnp.float32),
        "first_weight": gaussian(key_list[3], (3, 3, 3, CH, CH), (27 * CH) ** -0.5, 0.3125),
        "first_bias": gaussian(key_list[4], (CH,), 0.5, 3.0, jnp.float32),
        "second_weight": gaussian(key_list[5], (3, 3, 3, CH, CH), (27 * CH) ** -0.5, 0.3125),
        "second_bias": gaussian(key_list[6], (CH,), 0.5, 3.0, jnp.float32),
        "head_weight": gaussian(key_list[7], (CH,), CH ** -0.5, 1.5, jnp.float32),
        "mask_weight": gaussian(key_list[8], (CH, 9 * UP * UP), CH ** -0.5, 1.5, jnp.float32),
        "confidence": jnp.clip(jnp.exp(math.log(1.0) - 2.3025851 * jax.random.uniform(part_splits[9], (FULL_ROWS, FULL_COLS), jnp.float32) ** shard_levels(part_splits[9], (FULL_ROWS, FULL_COLS), ((0, 8),), -0.2, 0.2)), 0.1, 1.0),
    }


dual_step = 0.175
primal_step = 0.7
tv_bound = 0.3
cost_scale = 8.0
mask_scale = 3.0
highest_prec = lax.Precision.HIGHEST

def features(image, feat_weight):
    pixels = image.astype(jnp.float32) / 64.0 - 2.0
    row_count = image.shape[0] // UP
    col_count = image.shape[1] // UP
    patches = pixels.reshape(row_count, UP, col_count, UP).transpose(1, 3, 0, 2).reshape(UP * UP, row_count, col_count)
    return jnp.einsum('pc,prw->crw', feat_weight.astype(jnp.float32), patches, precision=highest_prec).astype(jnp.bfloat16)

def cost_volume(left_feat, right_feat, planes):
    col_count = right_feat.shape[2]
    padded = jnp.pad(right_feat, ((0, 0), (0, 0), (DSP, 0)))

    def take_plane(plane):
        return lax.dynamic_slice_in_dim(padded, (DSP - plane).astype(jnp.int32), col_count, 2)
    shifted = jax.vmap(take_plane)(planes)
    return (left_feat.astype(jnp.float32)[None] * shifted.astype(jnp.float32)).astype(jnp.bfloat16)

def conv_ref(values, weights, bias):
    plane_count, channels, row_count, col_count = values.shape
    padded = jnp.pad(values.astype(jnp.float32), ((1, 1), (0, 0), (1, 1), (1, 1)))
    summed = jnp.zeros((plane_count, weights.shape[4], row_count, col_count), jnp.float32)
    for shift_d in range(3):
        for shift_y in range(3):
            for shift_x in range(3):
                window = padded[shift_d:shift_d + plane_count, :, shift_y:shift_y + row_count, shift_x:shift_x + col_count]
                summed = summed + jnp.einsum('dirw,io->dorw', window, weights[shift_d, shift_y, shift_x].astype(jnp.float32))
    return summed + bias.astype(jnp.float32)[None, :, None, None]

def upsample(rimmed, left_feat, mask_weight):
    row_count = rimmed.shape[0] - 2
    col_count = rimmed.shape[1]
    logits = mask_scale * jnp.tanh(jnp.einsum('ck,crw->krw', mask_weight, left_feat.astype(jnp.float32), precision=highest_prec))
    expo = jnp.exp(logits).reshape(9, UP * UP, row_count, col_count)
    mixing = expo / lax.optimization_barrier(jnp.sum(expo, 0))
    widened = jnp.pad(rimmed, ((0, 0), (1, 1)))
    neighbours = jnp.stack([widened[shift_y:shift_y + row_count, shift_x:shift_x + col_count] for shift_y in range(3) for shift_x in range(3)])
    subpixel = lax.optimization_barrier(jnp.sum(mixing * neighbours[:, None], 0))
    return subpixel.reshape(UP, UP, row_count, col_count).transpose(2, 0, 3, 1).reshape(row_count * UP, col_count * UP)

def zero_row(values):
    return jnp.zeros_like(values[:1])

def tv_iter(current, target, fidelity, global_fine, row_total, fetch_below, fetch_above):
    primal, extrap, dual_x, dual_y = current
    below_row = fetch_below(extrap)
    downward = jnp.concatenate([extrap[1:], below_row], 0)
    inside = ((global_fine >= 0) & (global_fine < row_total - 1))[:, None]
    grad_y = jnp.where(inside, downward - extrap, 0.0)
    grad_x = jnp.concatenate([extrap[:, 1:] - extrap[:, :-1], jnp.zeros_like(extrap[:, :1])], 1)
    trial_x = dual_x + dual_step * grad_x
    trial_y = dual_y + dual_step * grad_y
    shrink = jnp.maximum(1.0, jnp.sqrt(trial_x * trial_x + trial_y * trial_y) / tv_bound)
    dual_x = trial_x / shrink
    dual_y = trial_y / shrink
    above_row = fetch_above(dual_y)
    upper = jnp.concatenate([above_row, dual_y[:-1]], 0)
    left_col = jnp.concatenate([jnp.zeros_like(dual_x[:, :1]), dual_x[:, :-1]], 1)
    divergence = dual_x - left_col + dual_y - upper
    updated = (primal + primal_step * divergence + primal_step * fidelity * target) / (1.0 + primal_step * fidelity)
    return (updated, 2.0 * updated - primal, dual_x, dual_y)

def reference(left_image, right_image, feat_weight, first_weight, first_bias, second_weight, second_bias, head_weight, mask_weight, confidence):
    left_feat = features(left_image, feat_weight)
    right_feat = features(right_image, feat_weight)
    planes = jnp.arange(DSP, dtype=jnp.int32)
    volume = cost_volume(left_feat, right_feat, planes)
    hidden = jax.nn.relu(conv_ref(volume, first_weight, first_bias)).astype(jnp.bfloat16)
    second = jax.nn.relu(conv_ref(hidden, second_weight, second_bias))
    raw_score = jnp.einsum('dorw,o->drw', second, head_weight, precision=highest_prec)
    match_cost = cost_scale * jnp.tanh(raw_score)
    expo = jnp.exp(-match_cost)
    plane_frac = planes.astype(jnp.float32) / DSP
    coarse = lax.optimization_barrier(jnp.sum(expo * plane_frac[:, None, None], 0)) / lax.optimization_barrier(jnp.sum(expo, 0))
    rimmed = jnp.pad(coarse, ((1, 1), (0, 0)))
    initial = upsample(rimmed, left_feat, mask_weight)
    row_total = initial.shape[0]
    global_fine = jnp.arange(row_total, dtype=jnp.int32)
    current = (initial, initial, jnp.zeros_like(initial), jnp.zeros_like(initial))
    for step_index in range(TV_ITERS):
        current = tv_iter(current, initial, confidence, global_fine, row_total, zero_row, zero_row)
    return (coarse, current[0])
```

```python
import functools

import jax
import jax.numpy as jnp
from jax import lax
from jax.experimental import pallas as pl
from jax.experimental.pallas import tpu as pltpu
from jax.sharding import PartitionSpec as P

DSP = 128
UP = 4
TV_ITERS = 8
REACH = 2

dual_step = 0.175
primal_step = 0.7
tv_bound = 0.3
cost_scale = 8.0
mask_scale = 3.0
highest_prec = lax.Precision.HIGHEST
f32 = jnp.float32
bf16 = jnp.bfloat16
CHUNK1 = 11
CHUNK2 = 8


def iota(shape, dim):
    return lax.broadcasted_iota(jnp.int32, shape, dim)


def one_hot(cond):
    return jnp.where(cond, 1.0, 0.0)


def dot(a, b, dims=((1,), (0,)), precision=None):
    return lax.dot_general(a, b, (dims, ((), ())), precision=precision, preferred_element_type=f32)


def column(row, groups):
    ch = row.shape[1]
    shape = (groups * ch, ch)
    return jnp.sum(
        jnp.where(iota(shape, 0) % ch == iota(shape, 1), jnp.broadcast_to(row, shape), 0.0),
        axis=1,
        keepdims=True,
    )


def split(value):
    high = value.astype(bf16)
    return high, (value - high.astype(f32)).astype(bf16)


def kernel(
    npix, ndisp,
    left_ref, right_ref, featw_ref, w1_ref, b1_ref, w2_ref, b2_ref, head_ref, mask_ref, conf_ref,
    coarse_ref, out_ref,
    rows_buf, part_buf, wt_buf, wmat_buf, col_buf, lr_buf, hid_buf, score_buf, mix_buf,
    rows_send, rows_recv, part_send, part_recv,
):
    fine_rows, fine_cols = left_ref.shape
    rows = fine_rows // UP
    cols = fine_cols // UP
    ch = featw_ref.shape[1]
    planes = DSP // ndisp
    pix = lax.axis_index("pix")
    disp = lax.axis_index("disp")
    start = disp * planes

    def target(k, dc):
        return {"pix": pix + k, "disp": lax.rem(disp + dc, ndisp)}

    def exists(k):
        return (pix + k >= 0) & (pix + k < npix)

    offsets = [k for k in range(-REACH, REACH + 1)]
    barrier = pltpu.get_barrier_semaphore()
    expected = jnp.int32(0)
    for k in offsets:
        for dc in range(ndisp):
            if k == 0 and dc == 0:
                continue

            @pl.when(exists(k))
            def _():
                pl.semaphore_signal(
                    barrier, inc=1, device_id=target(k, dc), device_id_type=pl.DeviceIdType.MESH
                )

            expected = expected + jnp.where(exists(k), 1, 0)

    block = UP * (cols // UP)
    wide = block // UP
    ii, oo = iota((block, block), 0), iota((block, block), 1)
    undo = one_hot((ii % UP == oo // wide) & (ii // UP == oo % wide)).astype(bf16)
    stacked = jnp.concatenate(
        [
            (left_ref[...] - 128).astype(f32) / 64.0,
            (right_ref[...] - 128).astype(f32) / 64.0,
            conf_ref[...],
            jnp.zeros((fine_rows, fine_cols), f32),
        ],
        axis=0,
    ).astype(bf16)
    tall = stacked.shape[0]
    blocks = fine_cols // block
    res = dot(
        jnp.concatenate([stacked[:, j * block : (j + 1) * block] for j in range(blocks)], axis=0),
        undo,
    )
    by_b = [
        jnp.concatenate(
            [res[j * tall : (j + 1) * tall, b * wide : (b + 1) * wide] for j in range(blocks)],
            axis=1,
        )
        for b in range(UP)
    ]
    patch_left, patch_right, conf_rows = [
        jnp.concatenate([v[n * fine_rows : (n + 1) * fine_rows] for v in by_b], axis=0)
        for n in range(3)
    ]
    patch_rows = UP * fine_rows
    pp, qq = iota((UP * UP, patch_rows), 0), iota((UP * UP, patch_rows), 1)
    pick = one_hot(pp == UP * (qq % UP) + qq // fine_rows)
    spread = dot(featw_ref[...], pick, ((0,), (0,)), highest_prec)
    spread = jnp.concatenate([spread] * rows, axis=0)
    rr, qq = iota(spread.shape, 0), iota(spread.shape, 1)
    spread = jnp.where(rr // ch == (qq % fine_rows) // UP, spread, 0.0)
    frows = rows * ch
    rows_buf[1, 0:frows, :] = dot(spread, patch_left, precision=highest_prec).astype(bf16)
    rows_buf[1, frows : 2 * frows, :] = dot(spread, patch_right, precision=highest_prec).astype(bf16)
    rows_buf[1, 2 * frows : 2 * frows + patch_rows, :] = conf_rows.astype(bf16)

    pl.semaphore_wait(barrier, expected)

    def rows_copy(k):
        return pltpu.make_async_remote_copy(
            src_ref=rows_buf.at[1],
            dst_ref=rows_buf.at[1 - k],
            send_sem=rows_send.at[1 + k],
            recv_sem=rows_recv.at[1 - k],
            device_id=target(k, 0),
            device_id_type=pl.DeviceIdType.MESH,
        )

    for k in (-1, 1):

        @pl.when(exists(k))
        def _():
            rows_copy(k).start()

        @pl.when(jnp.logical_not(exists(k)))
        def _():
            rows_buf[1 + k] = jnp.zeros(rows_buf.shape[1:], bf16)

    for n, w_ref in enumerate((w1_ref, w2_ref)):
        wt_buf[...] = jnp.zeros_like(wt_buf)
        for kd in range(3):
            for ky in range(3):
                for kx in range(3):
                    tap = w_ref[kd, ky, kx].astype(f32)
                    for pd in range(2):
                        for py in range(2):
                            row = ((kd + pd) * 4 + ky + py) * ch
                            col = (kx * 4 + pd * 2 + py) * ch
                            wt_buf[row : row + ch, col : col + ch] = tap
        wmat_buf[n] = wt_buf[...].T[: 12 * ch].astype(bf16)
    group = 4 * ch
    for n, ref in enumerate((b1_ref, b2_ref, head_ref)):
        col_buf[n] = jnp.broadcast_to(column(ref[...], 4), (group, cols))

    def rows_wait(k):
        return pltpu.make_async_remote_copy(
            src_ref=rows_buf.at[1],
            dst_ref=rows_buf.at[1 + k],
            send_sem=rows_send.at[1 + k],
            recv_sem=rows_recv.at[1 + k],
            device_id=target(k, 0),
            device_id_type=pl.DeviceIdType.MESH,
        )

    for k in (-1, 1):

        @pl.when(exists(k))
        def _():
            rows_wait(k).wait_recv()

    for slot in range(3):
        for side in range(2):
            lr_buf[side, slot * frows : (slot + 1) * frows, :] = rows_buf[
                slot, side * frows : (side + 1) * frows, :
            ].astype(f32)

    lane = iota((group, cols), 1)
    not_first = lane >= 1
    not_last = lane < cols - 1

    def conv(weights, values):
        acc = dot(weights, values)
        before = jnp.where(not_first, pltpu.roll(acc[0:group], 1, 1), 0.0)
        after = jnp.where(not_last, pltpu.roll(acc[2 * group :], cols - 1, 1), 0.0)
        return acc[group : 2 * group] + before + after

    def volume(plane):
        shift = lax.rem(plane + cols, cols)
        moved = pltpu.roll(lr_buf[1], shift, 1)
        keep = (iota(moved.shape, 1) >= plane) & (plane >= 0) & (plane < DSP)
        return jnp.where(keep, moved * lr_buf[0], 0.0).astype(bf16)

    vrows = 4 * ch
    half = 2 * ch

    def first(c, carry):
        base = c * (2 * CHUNK1)
        held = [volume(start - 2 + base), volume(start - 1 + base)]
        for j in range(CHUNK1):
            held = held[-2:] + [volume(start + base + 2 * j + n) for n in range(2)]
            for rb in range(2):
                values = jnp.concatenate([v[rb * half : rb * half + vrows] for v in held], axis=0)
                got = jnp.maximum(conv(wmat_buf[0], values) + col_buf[0], 0.0).astype(bf16)
                for pd in range(2):
                    hid_buf[base + 2 * j + pd, rb * half : (rb + 1) * half, :] = got[
                        pd * half : (pd + 1) * half
                    ]
        return carry

    lax.fori_loop(0, (planes // 2 + 1) // CHUNK1, first, 0)

    @pl.when(pix == 0)
    def _():
        hid_buf[:, 0:ch, :] = jnp.zeros((planes + 2, ch, cols), bf16)

    @pl.when(pix == npix - 1)
    def _():
        hid_buf[:, 3 * ch : 4 * ch, :] = jnp.zeros((planes + 2, ch, cols), bf16)

    @pl.when(disp == 0)
    def _():
        hid_buf[0] = jnp.zeros((4 * ch, cols), bf16)

    @pl.when(disp == ndisp - 1)
    def _():
        hid_buf[planes + 1] = jnp.zeros((4 * ch, cols), bf16)

    def second(c, carry):
        base = c * CHUNK2
        for j in range(CHUNK2):
            values = hid_buf[pl.ds(2 * (base + j), 4)].reshape(4 * vrows, cols)
            got = jnp.maximum(conv(wmat_buf[1], values) + col_buf[1], 0.0) * col_buf[2]
            score_buf[base + j] = jnp.sum(got.reshape(4, ch, cols), axis=1)
        return carry

    lax.fori_loop(0, planes // 2 // CHUNK2, second, 0)

    expo = jnp.exp(-cost_scale * jnp.tanh(score_buf[...]))
    shape = expo.shape
    plane = start + 2 * iota(shape, 0) + iota(shape, 1) // rows
    weight4 = jnp.sum(expo, axis=0)
    plane4 = jnp.sum(expo * (plane.astype(f32) / DSP), axis=0)
    mine = jnp.concatenate(
        [plane4[0:rows] + plane4[rows:], weight4[0:rows] + weight4[rows:], jnp.ones((4, cols), f32)],
        axis=0,
    )
    part_buf[REACH, disp] = mine

    def part_copy(k, dc):
        return pltpu.make_async_remote_copy(
            src_ref=part_buf.at[REACH, disp],
            dst_ref=part_buf.at[REACH - k, disp],
            send_sem=part_send.at[REACH + k, dc],
            recv_sem=part_recv.at[REACH - k, disp],
            device_id=target(k, dc),
            device_id_type=pl.DeviceIdType.MESH,
        )

    def part_wait(k, dc):
        core = lax.rem(disp + dc, ndisp)
        return pltpu.make_async_remote_copy(
            src_ref=part_buf.at[REACH, disp],
            dst_ref=part_buf.at[REACH + k, core],
            send_sem=part_send.at[REACH + k, dc],
            recv_sem=part_recv.at[REACH + k, core],
            device_id=target(k, dc),
            device_id_type=pl.DeviceIdType.MESH,
        )

    partners = [(k, dc) for k in (2, -2, 1, -1, 0) for dc in range(ndisp) if (k, dc) != (0, 0)]
    for k, dc in partners:

        @pl.when(exists(k))
        def _():
            part_copy(k, dc).start()

    for k in (-2, -1, 1, 2):

        @pl.when(jnp.logical_not(exists(k)))
        def _():
            for core in range(ndisp):
                part_buf[REACH + k, core] = jnp.where(iota((8, cols), 0) < rows, 0.0, 1.0)

    deep = 8
    taps = mask_ref.shape[1]
    cc, qq = iota((ch, deep * ch), 0), iota((ch, deep * ch), 1)
    tiled = dot(mask_ref[...], one_hot(cc == qq % ch), ((0,), (0,)), highest_prec)
    shape = (taps, deep, deep * ch)
    big = jnp.where(
        iota(shape, 1) == iota(shape, 2) // ch, jnp.broadcast_to(tiled[:, None, :], shape), 0.0
    ).reshape(taps * deep, deep * ch)
    none = jnp.zeros((ch, cols), bf16)
    lines = jnp.concatenate(
        [none] + [rows_buf[slot, 0:frows, :] for slot in range(3)] + [none], axis=0
    )
    big_high, big_low = split(big)
    logits = dot(
        jnp.concatenate([big_high, big_low], axis=1), jnp.concatenate([lines, lines], axis=0)
    )
    expo = jnp.exp(mask_scale * jnp.tanh(logits)).reshape(9, UP * UP, deep, cols)
    mix_buf[...] = expo * (1.0 / jnp.sum(expo, axis=0))[None]

    conf_all = jnp.concatenate(
        [rows_buf[slot, 2 * frows : 2 * frows + patch_rows, :] for slot in range(3)], axis=0
    )
    shape = (UP * UP * deep, 3 * patch_rows)
    to, fr = iota(shape, 0), iota(shape, 1)
    to_a, to_b, to_s = to // (UP * deep), (to // deep) % UP, to % deep
    fr_slot, fr_b, fr_r, fr_a = fr // patch_rows, (fr // fine_rows) % UP, (fr // UP) % rows, fr % UP
    place = one_hot((to_a == fr_a) & (to_b == fr_b) & (to_s - 1 == fr_slot * rows + fr_r))
    fidelity = dot(place.astype(bf16), conf_all).reshape(UP, UP, deep, cols)
    inverse = 1.0 / (1.0 + primal_step * fidelity)

    for k, dc in partners:

        @pl.when(exists(k))
        def _():
            part_wait(k, dc).wait_recv()

    total = part_buf[:, 0]
    for core in range(1, ndisp):
        total = total + part_buf[:, core]
    ratio = [total[n][0:rows] / total[n][rows : 2 * rows] for n in range(2 * REACH + 1)]
    coarse_ref[...] = ratio[REACH]
    coarse = jnp.concatenate([ratio[0][1:2]] + ratio[1:-1] + [ratio[-1][0:1]], axis=0)

    lane8 = iota((deep, cols), 1)
    lane_first, lane_last = lane8 >= 1, lane8 < cols - 1
    initial = None
    for ky in range(3):
        line = coarse if ky == 1 else pltpu.roll(coarse, (1 - ky) % deep, 0)
        for kx in range(3):
            if kx == 0:
                near = jnp.where(lane_first, pltpu.roll(line, 1, 1), 0.0)
            elif kx == 2:
                near = jnp.where(lane_last, pltpu.roll(line, cols - 1, 1), 0.0)
            else:
                near = line
            term = mix_buf[3 * ky + kx] * near[None]
            initial = term if initial is None else initial + term
    initial = initial.reshape(UP, UP, deep, cols)
    constant = primal_step * fidelity * initial * inverse

    line = pix * rows - 3 + iota((deep, cols), 0)
    inside = (line >= 0) & (line < npix * rows)
    inside_last = (line >= 0) & (line < npix * rows - 1)

    def tv(step, current):
        primal, extrap, dual_x, dual_y = current
        over = [
            jnp.where(lane_last, pltpu.roll(extrap[a, 0], cols - 1, 1) - extrap[a, UP - 1], 0.0)
            for a in range(UP)
        ]
        grad_x = jnp.concatenate(
            [extrap[:, 1:] - extrap[:, :-1], jnp.stack(over)[:, None]], axis=1
        )
        under = [
            jnp.where(inside_last, pltpu.roll(extrap[0, b], deep - 1, 0) - extrap[UP - 1, b], 0.0)
            for b in range(UP)
        ]
        grad_y = jnp.concatenate(
            [jnp.where(inside[None, None], extrap[1:] - extrap[:-1], 0.0), jnp.stack(under)[None]],
            axis=0,
        )
        trial_x = dual_x + dual_step * grad_x
        trial_y = dual_y + dual_step * grad_y
        square = jnp.maximum(trial_x * trial_x + trial_y * trial_y, 1e-30)
        shrink = jnp.minimum(1.0, tv_bound * lax.rsqrt(square))
        dual_x = trial_x * shrink
        dual_y = trial_y * shrink
        prior = [
            jnp.where(lane_first, pltpu.roll(dual_x[a, UP - 1], 1, 1), 0.0) for a in range(UP)
        ]
        left = jnp.concatenate([jnp.stack(prior)[:, None], dual_x[:, :-1]], axis=1)
        above = [pltpu.roll(dual_y[UP - 1, b], 1, 0) for b in range(UP)]
        upper = jnp.concatenate([jnp.stack(above)[None], dual_y[:-1]], axis=0)
        divergence = dual_x - left + dual_y - upper
        updated = (primal + primal_step * divergence) * inverse + constant
        return (updated, 2.0 * updated - primal, dual_x, dual_y)

    zeros = jnp.zeros_like(initial)
    result = lax.fori_loop(0, TV_ITERS, tv, (initial, initial, zeros, zeros))[0]

    shape = (fine_rows, UP * deep)
    to, fr = iota(shape, 0), iota(shape, 1)
    own = one_hot((to % UP == fr // deep) & (to // UP + 3 == fr % deep)).astype(bf16)
    pieces = []
    for b in range(UP):
        high, low = split(result[:, b].reshape(UP * deep, cols))
        pieces.append(jnp.concatenate([dot(own, high), dot(own, low)], axis=0).astype(bf16))
    redo = one_hot((oo % UP == ii // wide) & (oo // UP == ii % wide)).astype(bf16)
    for j in range(blocks):
        packed = jnp.concatenate([v[:, j * wide : (j + 1) * wide] for v in pieces], axis=1)
        both = dot(packed, redo)
        out_ref[:, j * block : (j + 1) * block] = both[0:fine_rows] + both[fine_rows:]

    for k in (-1, 1):

        @pl.when(exists(k))
        def _():
            rows_copy(k).wait_send()

    for k, dc in partners:

        @pl.when(exists(k))
        def _():
            part_copy(k, dc).wait_send()


def local(
    left_image, right_image, feat_weight, first_weight, first_bias,
    second_weight, second_bias, head_weight, mask_weight, confidence,
):
    npix, ndisp = lax.axis_size("pix"), lax.axis_size("disp")
    fine_rows, fine_cols = left_image.shape
    rows, cols = fine_rows // UP, fine_cols // UP
    ch = feat_weight.shape[1]
    planes = DSP // ndisp
    assert fine_rows == TV_ITERS and rows == 2
    vmem = pl.BlockSpec(memory_space=pltpu.VMEM)
    return pl.pallas_call(
        functools.partial(kernel, npix, ndisp),
        out_shape=(
            jax.ShapeDtypeStruct((rows, cols), f32),
            jax.ShapeDtypeStruct((fine_rows, fine_cols), f32),
        ),
        in_specs=[vmem] * 10,
        out_specs=(vmem, vmem),
        scratch_shapes=[
            pltpu.VMEM((3, 2 * rows * ch + UP * fine_rows, cols), bf16),
            pltpu.VMEM((2 * REACH + 1, ndisp, 8, cols), f32),
            pltpu.VMEM((16 * ch, 16 * ch), f32),
            pltpu.VMEM((2, 12 * ch, 16 * ch), bf16),
            pltpu.VMEM((3, 4 * ch, cols), f32),
            pltpu.VMEM((2, 3 * rows * ch, cols), f32),
            pltpu.VMEM((planes + 2, 4 * ch, cols), bf16),
            pltpu.VMEM((planes // 2, 2 * rows, cols), f32),
            pltpu.VMEM((9, UP * UP, 8, cols), f32),
            pltpu.SemaphoreType.DMA((3,)),
            pltpu.SemaphoreType.DMA((3,)),
            pltpu.SemaphoreType.DMA((2 * REACH + 1, ndisp)),
            pltpu.SemaphoreType.DMA((2 * REACH + 1, ndisp)),
        ],
        compiler_params=pltpu.CompilerParams(
            collective_id=0, has_side_effects=True, vmem_limit_bytes=40 * 1024 * 1024
        ),
    )(
        left_image, right_image, feat_weight, first_weight, first_bias[None],
        second_weight, second_bias[None], head_weight[None], mask_weight, confidence,
    )


def solution(mesh):
    placed = (
        P(("grp", "pix"), None),
        P(("grp", "pix"), None),
        P(),
        P(),
        P(),
        P(),
        P(),
        P(),
        P(),
        P(("grp", "pix"), None),
    )
    return jax.shard_map(
        local,
        mesh=mesh,
        in_specs=placed,
        out_specs=(P(("grp", "pix"), None), P(("grp", "pix"), None)),
        check_vma=False,
    )
```

```python
import functools

import jax
import jax.numpy as jnp
from jax import lax
from jax.experimental import pallas as pl
from jax.experimental.pallas import tpu as pltpu
from jax.sharding import PartitionSpec as P

DSP = 128
UP = 4
TV_ITERS = 8
REACH = 2

dual_step = 0.175
primal_step = 0.7
tv_bound = 0.3
cost_scale = 8.0
mask_scale = 3.0
highest_prec = lax.Precision.HIGHEST
f32 = jnp.float32
bf16 = jnp.bfloat16
LANES = 128
CHUNK1 = 11
CHUNK2 = 8


def iota(shape, dim):
    return lax.broadcasted_iota(jnp.int32, shape, dim)


def one_hot(cond):
    return jnp.where(cond, 1.0, 0.0)


def dot(a, b, dims=((1,), (0,)), precision=None):
    return lax.dot_general(a, b, (dims, ((), ())), precision=precision, preferred_element_type=f32)


def column(row, groups):
    ch = row.shape[1]
    shape = (groups * ch, ch)
    return jnp.sum(
        jnp.where(iota(shape, 0) % ch == iota(shape, 1), jnp.broadcast_to(row, shape), 0.0),
        axis=1,
        keepdims=True,
    )


def split(value):
    high = value.astype(bf16)
    return high, (value - high.astype(f32)).astype(bf16)


def kernel(
    npix, ndisp,
    left_hbm, right_hbm, featw_hbm, w1_hbm, b1_hbm, w2_hbm, b2_hbm, head_hbm, mask_hbm, conf_hbm,
    coarse_ref, out_ref,
    left_ref, right_ref, featw_ref, w1_ref, b1_ref, w2_ref, b2_ref, head_ref, mask_ref, conf_ref,
    load_sem,
    keep_buf, rows_buf, part_buf, wt_buf, wmat_buf, col_buf, lr_buf, hid_buf, score_buf, mix_buf,
    rows_send, rows_recv, part_send, part_recv,
):
    fine_rows, fine_cols = left_ref.shape
    rows = fine_rows // UP
    cols = fine_cols // UP
    ch = featw_ref.shape[1]
    planes = DSP // ndisp
    pix = lax.axis_index("pix")
    disp = lax.axis_index("disp")
    start = disp * planes

    def target(k, dc):
        return {"pix": pix + k, "disp": lax.rem(disp + dc, ndisp)}

    def exists(k):
        return (pix + k >= 0) & (pix + k < npix)

    loads = [
        pltpu.make_async_copy(src, dst, load_sem.at[n])
        for n, (src, dst) in enumerate(
            (
                (left_hbm, left_ref),
                (right_hbm, right_ref),
                (conf_hbm, conf_ref),
                (featw_hbm, featw_ref),
                (w1_hbm, w1_ref),
                (w2_hbm, w2_ref),
                (b1_hbm, b1_ref),
                (b2_hbm, b2_ref),
                (head_hbm, head_ref),
                (mask_hbm, mask_ref),
            )
        )
    ]
    for load in loads:
        load.start()

    offsets = [k for k in range(-REACH, REACH + 1)]
    barrier = pltpu.get_barrier_semaphore()
    expected = jnp.int32(0)
    for k in offsets:
        for dc in range(ndisp):
            if k == 0 and dc == 0:
                continue

            @pl.when(exists(k))
            def _():
                pl.semaphore_signal(
                    barrier, inc=1, device_id=target(k, dc), device_id_type=pl.DeviceIdType.MESH
                )

            expected = expected + jnp.where(exists(k), 1, 0)

    block = UP * (cols // UP)
    wide = block // UP
    ii, oo = iota((block, block), 0), iota((block, block), 1)
    undo = one_hot((ii % UP == oo // wide) & (ii // UP == oo % wide)).astype(bf16)
    for load in loads[:4]:
        load.wait()
    stacked = jnp.concatenate(
        [
            (left_ref[...] - 128).astype(f32) / 64.0,
            (right_ref[...] - 128).astype(f32) / 64.0,
            conf_ref[...],
            jnp.zeros((fine_rows, fine_cols), f32),
        ],
        axis=0,
    ).astype(bf16)
    tall = stacked.shape[0]
    blocks = fine_cols // block
    res = dot(
        jnp.concatenate([stacked[:, j * block : (j + 1) * block] for j in range(blocks)], axis=0),
        undo,
    )
    by_b = [
        jnp.concatenate(
            [res[j * tall : (j + 1) * tall, b * wide : (b + 1) * wide] for j in range(blocks)],
            axis=1,
        )
        for b in range(UP)
    ]
    patch_left, patch_right, conf_rows = [
        jnp.concatenate([v[n * fine_rows : (n + 1) * fine_rows] for v in by_b], axis=0)
        for n in range(3)
    ]
    patch_rows = UP * fine_rows
    pp, qq = iota((UP * UP, patch_rows), 0), iota((UP * UP, patch_rows), 1)
    pick = one_hot(pp == UP * (qq % UP) + qq // fine_rows)
    spread = dot(featw_ref[...], pick, ((0,), (0,)), highest_prec)
    spread = jnp.concatenate([spread] * rows, axis=0)
    rr, qq = iota(spread.shape, 0), iota(spread.shape, 1)
    spread = jnp.where(rr // ch == (qq % fine_rows) // UP, spread, 0.0)
    frows = rows * ch
    rows_buf[1, 0:frows, :] = dot(spread, patch_left, precision=highest_prec).astype(bf16)
    rows_buf[1, frows : 2 * frows, :] = dot(spread, patch_right, precision=highest_prec).astype(bf16)
    rows_buf[1, 2 * frows : 2 * frows + patch_rows, :] = conf_rows.astype(bf16)

    pl.semaphore_wait(barrier, expected)

    def rows_copy(k):
        return pltpu.make_async_remote_copy(
            src_ref=rows_buf.at[1],
            dst_ref=rows_buf.at[1 - k],
            send_sem=rows_send.at[1 + k],
            recv_sem=rows_recv.at[1 - k],
            device_id=target(k, 0),
            device_id_type=pl.DeviceIdType.MESH,
        )

    for k in (-1, 1):

        @pl.when(exists(k))
        def _():
            rows_copy(k).start()

        @pl.when(jnp.logical_not(exists(k)))
        def _():
            rows_buf[1 + k] = jnp.zeros(rows_buf.shape[1:], bf16)

    for load in loads[4:]:
        load.wait()

    for n, w_ref in enumerate((w1_ref, w2_ref)):
        wt_buf[...] = jnp.zeros_like(wt_buf)
        for kd in range(3):
            for ky in range(3):
                for kx in range(3):
                    tap = w_ref[kd, ky, kx].astype(f32)
                    for pd in range(2):
                        for py in range(2):
                            row = ((kd + pd) * 4 + ky + py) * ch
                            col = (kx * 4 + pd * 2 + py) * ch
                            wt_buf[row : row + ch, col : col + ch] = tap
        wmat_buf[n] = wt_buf[...].T[: 12 * ch].astype(bf16)
    group = 4 * ch
    for n, ref in enumerate((b1_ref, b2_ref, head_ref)):
        col_buf[n] = jnp.broadcast_to(column(ref[...], 4), (group, cols))

    def rows_wait(k):
        return pltpu.make_async_remote_copy(
            src_ref=rows_buf.at[1],
            dst_ref=rows_buf.at[1 + k],
            send_sem=rows_send.at[1 + k],
            recv_sem=rows_recv.at[1 + k],
            device_id=target(k, 0),
            device_id_type=pl.DeviceIdType.MESH,
        )

    for k in (-1, 1):

        @pl.when(exists(k))
        def _():
            rows_wait(k).wait_recv()

    for slot in range(3):
        for side in range(2):
            lr_buf[side, slot * frows : (slot + 1) * frows, :] = rows_buf[
                slot, side * frows : (side + 1) * frows, :
            ].astype(f32)

    lane = iota((group, LANES), 1)
    not_first = lane >= 1
    not_last = lane < LANES - 1

    def conv(weights, values):
        acc = dot(weights, values)
        moved_right, moved_left = {}, {}
        parts = []
        for n in range(cols // LANES):
            at = slice(n * LANES, (n + 1) * LANES)
            moved_right[n] = pltpu.roll(acc[0:group, at], 1, 1)
            moved_left[n] = pltpu.roll(acc[2 * group :, at], LANES - 1, 1)
        for n in range(cols // LANES):
            at = slice(n * LANES, (n + 1) * LANES)
            before = jnp.where(not_first, moved_right[n], moved_right.get(n - 1, 0.0))
            after = jnp.where(not_last, moved_left[n], moved_left.get(n + 1, 0.0))
            parts.append(acc[group : 2 * group, at] + before + after)
        return jnp.concatenate(parts, axis=1)

    def volume(plane):
        shift = lax.rem(plane + cols, cols)
        moved = pltpu.roll(lr_buf[1], shift, 1)
        keep = (iota(moved.shape, 1) >= plane) & (plane >= 0) & (plane < DSP)
        return jnp.where(keep, moved * lr_buf[0], 0.0).astype(bf16)

    vrows = 4 * ch
    half = 2 * ch

    left_rows = lr_buf[0].astype(bf16)
    keep_buf[...] = one_hot(iota(keep_buf.shape, 1) >= 1).astype(bf16)

    def first(c, carry):
        base = c * (2 * CHUNK1)
        held, moved = list(carry[:2]), carry[2]
        for j in range(CHUNK1):
            held = held[-2:]
            for n in range(2):
                held.append(moved * left_rows)
                inside = (start + base + 2 * j + n + 1 < DSP).astype(f32).astype(bf16)
                moved = pltpu.roll(moved, 1, 1) * (keep_buf[...] * inside)
            for rb in range(2):
                values = jnp.concatenate([v[rb * half : rb * half + vrows] for v in held], axis=0)
                got = jnp.maximum(conv(wmat_buf[0], values) + col_buf[0], 0.0).astype(bf16)
                for pd in range(2):
                    hid_buf[base + 2 * j + pd, rb * half : (rb + 1) * half, :] = got[
                        pd * half : (pd + 1) * half
                    ]
        return (held[-2], held[-1], moved)

    opening = jnp.where(
        iota(lr_buf.shape[1:], 1) >= start, pltpu.roll(lr_buf[1], start, 1), 0.0
    ).astype(bf16)
    lax.fori_loop(
        0,
        (planes // 2 + 1) // CHUNK1,
        first,
        (volume(start - 2), volume(start - 1), opening),
    )

    @pl.when(pix == 0)
    def _():
        hid_buf[:, 0:ch, :] = jnp.zeros((planes + 2, ch, cols), bf16)

    @pl.when(pix == npix - 1)
    def _():
        hid_buf[:, 3 * ch : 4 * ch, :] = jnp.zeros((planes + 2, ch, cols), bf16)

    @pl.when(disp == 0)
    def _():
        hid_buf[0] = jnp.zeros((4 * ch, cols), bf16)

    @pl.when(disp == ndisp - 1)
    def _():
        hid_buf[planes + 1] = jnp.zeros((4 * ch, cols), bf16)

    def second(c, carry):
        base = c * CHUNK2
        for j in range(CHUNK2):
            values = hid_buf[pl.ds(2 * (base + j), 4)].reshape(4 * vrows, cols)
            got = jnp.maximum(conv(wmat_buf[1], values) + col_buf[1], 0.0) * col_buf[2]
            score_buf[base + j] = jnp.sum(got.reshape(4, ch, cols), axis=1)
        return carry

    lax.fori_loop(0, planes // 2 // CHUNK2, second, 0)

    expo = jnp.exp(-cost_scale * jnp.tanh(score_buf[...]))
    shape = expo.shape
    plane = start + 2 * iota(shape, 0) + iota(shape, 1) // rows
    weight4 = jnp.sum(expo, axis=0)
    plane4 = jnp.sum(expo * (plane.astype(f32) / DSP), axis=0)
    mine = jnp.concatenate(
        [plane4[0:rows] + plane4[rows:], weight4[0:rows] + weight4[rows:], jnp.ones((4, cols), f32)],
        axis=0,
    )
    part_buf[REACH, disp] = mine

    def part_copy(k, dc):
        return pltpu.make_async_remote_copy(
            src_ref=part_buf.at[REACH, disp],
            dst_ref=part_buf.at[REACH - k, disp],
            send_sem=part_send.at[REACH + k, dc],
            recv_sem=part_recv.at[REACH - k, disp],
            device_id=target(k, dc),
            device_id_type=pl.DeviceIdType.MESH,
        )

    def part_wait(k, dc):
        core = lax.rem(disp + dc, ndisp)
        return pltpu.make_async_remote_copy(
            src_ref=part_buf.at[REACH, disp],
            dst_ref=part_buf.at[REACH + k, core],
            send_sem=part_send.at[REACH + k, dc],
            recv_sem=part_recv.at[REACH + k, core],
            device_id=target(k, dc),
            device_id_type=pl.DeviceIdType.MESH,
        )

    partners = [(k, dc) for k in (2, -2, 1, -1, 0) for dc in range(ndisp) if (k, dc) != (0, 0)]
    for k, dc in partners:

        @pl.when(exists(k))
        def _():
            part_copy(k, dc).start()

    for k in (-2, -1, 1, 2):

        @pl.when(jnp.logical_not(exists(k)))
        def _():
            for core in range(ndisp):
                part_buf[REACH + k, core] = jnp.where(iota((8, cols), 0) < rows, 0.0, 1.0)

    deep = 8
    taps = mask_ref.shape[1]
    cc, qq = iota((ch, deep * ch), 0), iota((ch, deep * ch), 1)
    tiled = dot(mask_ref[...], one_hot(cc == qq % ch), ((0,), (0,)), highest_prec)
    shape = (taps, deep, deep * ch)
    big = jnp.where(
        iota(shape, 1) == iota(shape, 2) // ch, jnp.broadcast_to(tiled[:, None, :], shape), 0.0
    ).reshape(taps * deep, deep * ch)
    none = jnp.zeros((ch, cols), bf16)
    lines = jnp.concatenate(
        [none] + [rows_buf[slot, 0:frows, :] for slot in range(3)] + [none], axis=0
    )
    big_high, big_low = split(big)
    logits = dot(
        jnp.concatenate([big_high, big_low], axis=1), jnp.concatenate([lines, lines], axis=0)
    )
    expo = jnp.exp(mask_scale * jnp.tanh(logits)).reshape(9, UP * UP, deep, cols)
    mix_buf[...] = expo * (1.0 / jnp.sum(expo, axis=0))[None]

    conf_all = jnp.concatenate(
        [rows_buf[slot, 2 * frows : 2 * frows + patch_rows, :] for slot in range(3)], axis=0
    )
    shape = (UP * UP * deep, 3 * patch_rows)
    to, fr = iota(shape, 0), iota(shape, 1)
    to_a, to_b, to_s = to // (UP * deep), (to // deep) % UP, to % deep
    fr_slot, fr_b, fr_r, fr_a = fr // patch_rows, (fr // fine_rows) % UP, (fr // UP) % rows, fr % UP
    place = one_hot((to_a == fr_a) & (to_b == fr_b) & (to_s - 1 == fr_slot * rows + fr_r))
    fidelity = dot(place.astype(bf16), conf_all).reshape(UP, UP, deep, cols)
    inverse = 1.0 / (1.0 + primal_step * fidelity)

    for k, dc in partners:

        @pl.when(exists(k))
        def _():
            part_wait(k, dc).wait_recv()

    total = part_buf[:, 0]
    for core in range(1, ndisp):
        total = total + part_buf[:, core]
    ratio = [total[n][0:rows] / total[n][rows : 2 * rows] for n in range(2 * REACH + 1)]
    coarse_ref[...] = ratio[REACH]
    coarse = jnp.concatenate([ratio[0][1:2]] + ratio[1:-1] + [ratio[-1][0:1]], axis=0)

    lane8 = iota((deep, cols), 1)
    lane_first, lane_last = lane8 >= 1, lane8 < cols - 1
    initial = None
    for ky in range(3):
        line = coarse if ky == 1 else pltpu.roll(coarse, (1 - ky) % deep, 0)
        for kx in range(3):
            if kx == 0:
                near = jnp.where(lane_first, pltpu.roll(line, 1, 1), 0.0)
            elif kx == 2:
                near = jnp.where(lane_last, pltpu.roll(line, cols - 1, 1), 0.0)
            else:
                near = line
            term = mix_buf[3 * ky + kx] * near[None]
            initial = term if initial is None else initial + term
    initial = initial.reshape(UP, UP, deep, cols)
    constant = primal_step * fidelity * initial * inverse

    line = pix * rows - 3 + iota((deep, cols), 0)
    inside = (line >= 0) & (line < npix * rows)
    inside_last = (line >= 0) & (line < npix * rows - 1)

    def tv(step, current):
        primal, extrap, dual_x, dual_y = current
        over = [
            jnp.where(lane_last, pltpu.roll(extrap[a, 0], cols - 1, 1) - extrap[a, UP - 1], 0.0)
            for a in range(UP)
        ]
        grad_x = jnp.concatenate(
            [extrap[:, 1:] - extrap[:, :-1], jnp.stack(over)[:, None]], axis=1
        )
        under = [
            jnp.where(inside_last, pltpu.roll(extrap[0, b], deep - 1, 0) - extrap[UP - 1, b], 0.0)
            for b in range(UP)
        ]
        grad_y = jnp.concatenate(
            [jnp.where(inside[None, None], extrap[1:] - extrap[:-1], 0.0), jnp.stack(under)[None]],
            axis=0,
        )
        trial_x = dual_x + dual_step * grad_x
        trial_y = dual_y + dual_step * grad_y
        square = jnp.maximum(trial_x * trial_x + trial_y * trial_y, 1e-30)
        shrink = jnp.minimum(1.0, tv_bound * lax.rsqrt(square))
        dual_x = trial_x * shrink
        dual_y = trial_y * shrink
        prior = [
            jnp.where(lane_first, pltpu.roll(dual_x[a, UP - 1], 1, 1), 0.0) for a in range(UP)
        ]
        left = jnp.concatenate([jnp.stack(prior)[:, None], dual_x[:, :-1]], axis=1)
        above = [pltpu.roll(dual_y[UP - 1, b], 1, 0) for b in range(UP)]
        upper = jnp.concatenate([jnp.stack(above)[None], dual_y[:-1]], axis=0)
        divergence = dual_x - left + dual_y - upper
        updated = (primal + primal_step * divergence) * inverse + constant
        return (updated, 2.0 * updated - primal, dual_x, dual_y)

    zeros = jnp.zeros_like(initial)
    result = lax.fori_loop(0, TV_ITERS, tv, (initial, initial, zeros, zeros))[0]

    shape = (fine_rows, UP * deep)
    to, fr = iota(shape, 0), iota(shape, 1)
    own = one_hot((to % UP == fr // deep) & (to // UP + 3 == fr % deep)).astype(bf16)
    pieces = []
    for b in range(UP):
        high, low = split(result[:, b].reshape(UP * deep, cols))
        pieces.append(jnp.concatenate([dot(own, high), dot(own, low)], axis=0).astype(bf16))
    redo = one_hot((oo % UP == ii // wide) & (oo // UP == ii % wide)).astype(bf16)
    for j in range(blocks):
        packed = jnp.concatenate([v[:, j * wide : (j + 1) * wide] for v in pieces], axis=1)
        both = dot(packed, redo)
        out_ref[:, j * block : (j + 1) * block] = both[0:fine_rows] + both[fine_rows:]

    for k in (-1, 1):

        @pl.when(exists(k))
        def _():
            rows_copy(k).wait_send()

    for k, dc in partners:

        @pl.when(exists(k))
        def _():
            part_copy(k, dc).wait_send()


def local(
    left_image, right_image, feat_weight, first_weight, first_bias,
    second_weight, second_bias, head_weight, mask_weight, confidence,
):
    npix, ndisp = lax.axis_size("pix"), lax.axis_size("disp")
    fine_rows, fine_cols = left_image.shape
    rows, cols = fine_rows // UP, fine_cols // UP
    ch = feat_weight.shape[1]
    planes = DSP // ndisp
    assert fine_rows == TV_ITERS and rows == 2
    vmem = pl.BlockSpec(memory_space=pltpu.VMEM)
    args = (
        left_image, right_image, feat_weight, first_weight, first_bias[None],
        second_weight, second_bias[None], head_weight[None], mask_weight, confidence,
    )
    return pl.pallas_call(
        functools.partial(kernel, npix, ndisp),
        out_shape=(
            jax.ShapeDtypeStruct((rows, cols), f32),
            jax.ShapeDtypeStruct((fine_rows, fine_cols), f32),
        ),
        in_specs=[pl.BlockSpec(memory_space=pltpu.HBM)] * 10,
        out_specs=(vmem, vmem),
        scratch_shapes=[pltpu.VMEM(arg.shape, arg.dtype) for arg in args]
        + [
            pltpu.SemaphoreType.DMA((len(args),)),
            pltpu.VMEM((3 * rows * ch, cols), bf16),
            pltpu.VMEM((3, 2 * rows * ch + UP * fine_rows, cols), bf16),
            pltpu.VMEM((2 * REACH + 1, ndisp, 8, cols), f32),
            pltpu.VMEM((16 * ch, 16 * ch), f32),
            pltpu.VMEM((2, 12 * ch, 16 * ch), bf16),
            pltpu.VMEM((3, 4 * ch, cols), f32),
            pltpu.VMEM((2, 3 * rows * ch, cols), f32),
            pltpu.VMEM((planes + 2, 4 * ch, cols), bf16),
            pltpu.VMEM((planes // 2, 2 * rows, cols), f32),
            pltpu.VMEM((9, UP * UP, 8, cols), f32),
            pltpu.SemaphoreType.DMA((3,)),
            pltpu.SemaphoreType.DMA((3,)),
            pltpu.SemaphoreType.DMA((2 * REACH + 1, ndisp)),
            pltpu.SemaphoreType.DMA((2 * REACH + 1, ndisp)),
        ],
        compiler_params=pltpu.CompilerParams(
            collective_id=0, has_side_effects=True, vmem_limit_bytes=56 * 1024 * 1024
        ),
    )(*args)


def solution(mesh):
    placed = (
        P(("grp", "pix"), None),
        P(("grp", "pix"), None),
        P(),
        P(),
        P(),
        P(),
        P(),
        P(),
        P(),
        P(("grp", "pix"), None),
    )
    return jax.shard_map(
        local,
        mesh=mesh,
        in_specs=placed,
        out_specs=(P(("grp", "pix"), None), P(("grp", "pix"), None)),
        check_vma=False,
    )
```

```python
import functools

import jax
import jax.numpy as jnp
from jax import lax
from jax.experimental import pallas as pl
from jax.experimental.pallas import tpu as pltpu
from jax.sharding import PartitionSpec as P

DSP = 128
UP = 4
TV_ITERS = 8
REACH = 2

dual_step = 0.175
primal_step = 0.7
tv_bound = 0.3
cost_scale = 8.0
mask_scale = 3.0
highest_prec = lax.Precision.HIGHEST
f32 = jnp.float32
bf16 = jnp.bfloat16
LANES = 128
CHUNK1 = 11
CHUNK2 = 8


def iota(shape, dim):
    return lax.broadcasted_iota(jnp.int32, shape, dim)


def one_hot(cond):
    return jnp.where(cond, 1.0, 0.0)


def dot(a, b, dims=((1,), (0,)), precision=None):
    return lax.dot_general(a, b, (dims, ((), ())), precision=precision, preferred_element_type=f32)


def column(row, groups):
    ch = row.shape[1]
    shape = (groups * ch, ch)
    return jnp.sum(
        jnp.where(iota(shape, 0) % ch == iota(shape, 1), jnp.broadcast_to(row, shape), 0.0),
        axis=1,
        keepdims=True,
    )


def split(value):
    high = value.astype(bf16)
    return high, (value - high.astype(f32)).astype(bf16)


def kernel(
    npix, ndisp,
    left_hbm, right_hbm, featw_hbm, w1_hbm, b1_hbm, w2_hbm, b2_hbm, head_hbm, mask_hbm, conf_hbm,
    coarse_ref, out_ref,
    left_ref, right_ref, featw_ref, w1_ref, b1_ref, w2_ref, b2_ref, head_ref, mask_ref, conf_ref,
    load_sem,
    keep_buf, rows_buf, part_buf, wt_buf, wmat_buf, col_buf, lr_buf, hid_buf, score_buf, mix_buf,
    rows_send, rows_recv, part_send, part_recv,
):
    fine_rows, fine_cols = left_ref.shape
    rows = fine_rows // UP
    cols = fine_cols // UP
    ch = featw_ref.shape[1]
    planes = DSP // ndisp
    pix = lax.axis_index("pix")
    disp = lax.axis_index("disp")
    start = disp * planes

    def target(k, dc):
        return {"pix": pix + k, "disp": lax.rem(disp + dc, ndisp)}

    def exists(k):
        return (pix + k >= 0) & (pix + k < npix)

    loads = [
        pltpu.make_async_copy(src, dst, load_sem.at[n])
        for n, (src, dst) in enumerate(
            (
                (left_hbm, left_ref),
                (right_hbm, right_ref),
                (conf_hbm, conf_ref),
                (featw_hbm, featw_ref),
                (w1_hbm, w1_ref),
                (w2_hbm, w2_ref),
                (b1_hbm, b1_ref),
                (b2_hbm, b2_ref),
                (head_hbm, head_ref),
                (mask_hbm, mask_ref),
            )
        )
    ]
    for load in loads:
        load.start()

    offsets = [k for k in range(-REACH, REACH + 1)]
    barrier = pltpu.get_barrier_semaphore()
    expected = jnp.int32(0)
    for k in offsets:
        for dc in range(ndisp):
            if k == 0 and dc == 0:
                continue

            @pl.when(exists(k))
            def _():
                pl.semaphore_signal(
                    barrier, inc=1, device_id=target(k, dc), device_id_type=pl.DeviceIdType.MESH
                )

            expected = expected + jnp.where(exists(k), 1, 0)

    block = UP * (cols // UP)
    wide = block // UP
    ii, oo = iota((block, block), 0), iota((block, block), 1)
    undo = one_hot((ii % UP == oo // wide) & (ii // UP == oo % wide)).astype(bf16)
    for load in loads[:4]:
        load.wait()
    stacked = jnp.concatenate(
        [
            (left_ref[...] - 128).astype(f32) / 64.0,
            (right_ref[...] - 128).astype(f32) / 64.0,
            conf_ref[...],
            jnp.zeros((fine_rows, fine_cols), f32),
        ],
        axis=0,
    ).astype(bf16)
    tall = stacked.shape[0]
    blocks = fine_cols // block
    res = dot(
        jnp.concatenate([stacked[:, j * block : (j + 1) * block] for j in range(blocks)], axis=0),
        undo,
    )
    by_b = [
        jnp.concatenate(
            [res[j * tall : (j + 1) * tall, b * wide : (b + 1) * wide] for j in range(blocks)],
            axis=1,
        )
        for b in range(UP)
    ]
    patch_left, patch_right, conf_rows = [
        jnp.concatenate([v[n * fine_rows : (n + 1) * fine_rows] for v in by_b], axis=0)
        for n in range(3)
    ]
    patch_rows = UP * fine_rows
    pp, qq = iota((UP * UP, patch_rows), 0), iota((UP * UP, patch_rows), 1)
    pick = one_hot(pp == UP * (qq % UP) + qq // fine_rows)
    spread = dot(featw_ref[...], pick, ((0,), (0,)), highest_prec)
    spread = jnp.concatenate([spread] * rows, axis=0)
    rr, qq = iota(spread.shape, 0), iota(spread.shape, 1)
    spread = jnp.where(rr // ch == (qq % fine_rows) // UP, spread, 0.0)
    frows = rows * ch
    rows_buf[1, 0:frows, :] = dot(spread, patch_left, precision=highest_prec).astype(bf16)
    rows_buf[1, frows : 2 * frows, :] = dot(spread, patch_right, precision=highest_prec).astype(bf16)
    rows_buf[1, 2 * frows : 2 * frows + patch_rows, :] = conf_rows.astype(bf16)

    pl.semaphore_wait(barrier, expected)

    def rows_copy(k):
        return pltpu.make_async_remote_copy(
            src_ref=rows_buf.at[1],
            dst_ref=rows_buf.at[1 - k],
            send_sem=rows_send.at[1 + k],
            recv_sem=rows_recv.at[1 - k],
            device_id=target(k, 0),
            device_id_type=pl.DeviceIdType.MESH,
        )

    for k in (-1, 1):

        @pl.when(exists(k))
        def _():
            rows_copy(k).start()

        @pl.when(jnp.logical_not(exists(k)))
        def _():
            rows_buf[1 + k] = jnp.zeros(rows_buf.shape[1:], bf16)

    for load in loads[4:]:
        load.wait()

    for n, w_ref in enumerate((w1_ref, w2_ref)):
        wt_buf[...] = jnp.zeros_like(wt_buf)
        for kd in range(3):
            for ky in range(3):
                for kx in range(3):
                    tap = w_ref[kd, ky, kx].astype(f32)
                    for pd in range(2):
                        for py in range(2):
                            row = ((kd + pd) * 4 + ky + py) * ch
                            col = (kx * 4 + pd * 2 + py) * ch
                            wt_buf[row : row + ch, col : col + ch] = tap
        wmat_buf[n] = wt_buf[...].T[: 12 * ch].astype(bf16)
    group = 4 * ch
    for n, ref in enumerate((b1_ref, b2_ref, head_ref)):
        col_buf[n] = jnp.broadcast_to(column(ref[...], 4), (group, cols))

    def rows_wait(k):
        return pltpu.make_async_remote_copy(
            src_ref=rows_buf.at[1],
            dst_ref=rows_buf.at[1 + k],
            send_sem=rows_send.at[1 + k],
            recv_sem=rows_recv.at[1 + k],
            device_id=target(k, 0),
            device_id_type=pl.DeviceIdType.MESH,
        )

    for k in (-1, 1):

        @pl.when(exists(k))
        def _():
            rows_wait(k).wait_recv()

    for slot in range(3):
        for side in range(2):
            lr_buf[side, slot * frows : (slot + 1) * frows, :] = rows_buf[
                slot, side * frows : (side + 1) * frows, :
            ].astype(f32)

    lane = iota((group, LANES), 1)
    not_first = lane >= 1
    not_last = lane < LANES - 1

    def conv(weights, values):
        acc = dot(weights, values)
        moved_right, moved_left = {}, {}
        parts = []
        for n in range(cols // LANES):
            at = slice(n * LANES, (n + 1) * LANES)
            moved_right[n] = pltpu.roll(acc[0:group, at], 1, 1)
            moved_left[n] = pltpu.roll(acc[2 * group :, at], LANES - 1, 1)
        for n in range(cols // LANES):
            at = slice(n * LANES, (n + 1) * LANES)
            before = jnp.where(not_first, moved_right[n], moved_right.get(n - 1, 0.0))
            after = jnp.where(not_last, moved_left[n], moved_left.get(n + 1, 0.0))
            parts.append(acc[group : 2 * group, at] + before + after)
        return jnp.concatenate(parts, axis=1)

    def volume(plane):
        shift = lax.rem(plane + cols, cols)
        moved = pltpu.roll(lr_buf[1], shift, 1)
        keep = (iota(moved.shape, 1) >= plane) & (plane >= 0) & (plane < DSP)
        return jnp.where(keep, moved * lr_buf[0], 0.0).astype(bf16)

    vrows = 4 * ch
    half = 2 * ch

    left_rows = lr_buf[0].astype(bf16)
    keep_buf[...] = one_hot(iota(keep_buf.shape, 1) >= 1).astype(bf16)

    def first(c, carry):
        base = c * (2 * CHUNK1)
        held, moved = list(carry[:2]), carry[2]
        for j in range(CHUNK1):
            held = held[-2:]
            for n in range(2):
                held.append(moved * left_rows)
                inside = (start + base + 2 * j + n + 1 < DSP).astype(f32).astype(bf16)
                moved = pltpu.roll(moved, 1, 1) * (keep_buf[...] * inside)
            for rb in range(2):
                values = jnp.concatenate([v[rb * half : rb * half + vrows] for v in held], axis=0)
                got = jnp.maximum(conv(wmat_buf[0], values) + col_buf[0], 0.0).astype(bf16)
                for pd in range(2):
                    hid_buf[base + 2 * j + pd, rb * half : (rb + 1) * half, :] = got[
                        pd * half : (pd + 1) * half
                    ]
        return (held[-2], held[-1], moved)

    opening = jnp.where(
        iota(lr_buf.shape[1:], 1) >= start, pltpu.roll(lr_buf[1], start, 1), 0.0
    ).astype(bf16)
    lax.fori_loop(
        0,
        (planes // 2 + 1) // CHUNK1,
        first,
        (volume(start - 2), volume(start - 1), opening),
    )

    @pl.when(pix == 0)
    def _():
        hid_buf[:, 0:ch, :] = jnp.zeros((planes + 2, ch, cols), bf16)

    @pl.when(pix == npix - 1)
    def _():
        hid_buf[:, 3 * ch : 4 * ch, :] = jnp.zeros((planes + 2, ch, cols), bf16)

    @pl.when(disp == 0)
    def _():
        hid_buf[0] = jnp.zeros((4 * ch, cols), bf16)

    @pl.when(disp == ndisp - 1)
    def _():
        hid_buf[planes + 1] = jnp.zeros((4 * ch, cols), bf16)

    def second(c, carry):
        base = c * CHUNK2
        for j in range(CHUNK2):
            values = hid_buf[pl.ds(2 * (base + j), 4)].reshape(4 * vrows, cols)
            got = jnp.maximum(conv(wmat_buf[1], values) + col_buf[1], 0.0) * col_buf[2]
            score_buf[base + j] = jnp.sum(got.reshape(4, ch, cols), axis=1)
        return carry

    lax.fori_loop(0, planes // 2 // CHUNK2, second, 0)

    expo = jnp.exp(-cost_scale * jnp.tanh(score_buf[...]))
    shape = expo.shape
    plane = start + 2 * iota(shape, 0) + iota(shape, 1) // rows
    weight4 = jnp.sum(expo, axis=0)
    plane4 = jnp.sum(expo * (plane.astype(f32) / DSP), axis=0)
    mine = jnp.concatenate(
        [plane4[0:rows] + plane4[rows:], weight4[0:rows] + weight4[rows:], jnp.ones((4, cols), f32)],
        axis=0,
    )
    part_buf[REACH, disp] = mine

    def part_copy(k, dc):
        return pltpu.make_async_remote_copy(
            src_ref=part_buf.at[REACH, disp],
            dst_ref=part_buf.at[REACH - k, disp],
            send_sem=part_send.at[REACH + k, dc],
            recv_sem=part_recv.at[REACH - k, disp],
            device_id=target(k, dc),
            device_id_type=pl.DeviceIdType.MESH,
        )

    def part_wait(k, dc):
        core = lax.rem(disp + dc, ndisp)
        return pltpu.make_async_remote_copy(
            src_ref=part_buf.at[REACH, disp],
            dst_ref=part_buf.at[REACH + k, core],
            send_sem=part_send.at[REACH + k, dc],
            recv_sem=part_recv.at[REACH + k, core],
            device_id=target(k, dc),
            device_id_type=pl.DeviceIdType.MESH,
        )

    partners = [(k, dc) for k in (2, -2, 1, -1, 0) for dc in range(ndisp) if (k, dc) != (0, 0)]
    for k, dc in partners:

        @pl.when(exists(k))
        def _():
            part_copy(k, dc).start()

    for k in (-2, -1, 1, 2):

        @pl.when(jnp.logical_not(exists(k)))
        def _():
            for core in range(ndisp):
                part_buf[REACH + k, core] = jnp.where(iota((8, cols), 0) < rows, 0.0, 1.0)

    deep = 8
    taps = mask_ref.shape[1]
    cc, qq = iota((ch, deep * ch), 0), iota((ch, deep * ch), 1)
    tiled = dot(mask_ref[...], one_hot(cc == qq % ch), ((0,), (0,)), highest_prec)
    shape = (taps, deep, deep * ch)
    big = jnp.where(
        iota(shape, 1) == iota(shape, 2) // ch, jnp.broadcast_to(tiled[:, None, :], shape), 0.0
    ).reshape(taps * deep, deep * ch)
    none = jnp.zeros((ch, cols), bf16)
    lines = jnp.concatenate(
        [none] + [rows_buf[slot, 0:frows, :] for slot in range(3)] + [none], axis=0
    )
    big_high, big_low = split(big)
    logits = dot(
        jnp.concatenate([big_high, big_low], axis=1), jnp.concatenate([lines, lines], axis=0)
    )
    expo = jnp.exp(mask_scale * jnp.tanh(logits)).reshape(9, UP * UP, deep, cols)
    mix_buf[...] = expo * (1.0 / jnp.sum(expo, axis=0))[None]

    conf_all = jnp.concatenate(
        [rows_buf[slot, 2 * frows : 2 * frows + patch_rows, :] for slot in range(3)], axis=0
    )
    shape = (UP * UP * deep, 3 * patch_rows)
    to, fr = iota(shape, 0), iota(shape, 1)
    to_a, to_b, to_s = to // (UP * deep), (to // deep) % UP, to % deep
    fr_slot, fr_b, fr_r, fr_a = fr // patch_rows, (fr // fine_rows) % UP, (fr // UP) % rows, fr % UP
    place = one_hot((to_a == fr_a) & (to_b == fr_b) & (to_s - 1 == fr_slot * rows + fr_r))
    fidelity = dot(place.astype(bf16), conf_all).reshape(UP, UP, deep, cols)
    inverse = 1.0 / (1.0 + primal_step * fidelity)

    for k, dc in partners:

        @pl.when(exists(k))
        def _():
            part_wait(k, dc).wait_recv()

    total = part_buf[:, 0]
    for core in range(1, ndisp):
        total = total + part_buf[:, core]
    ratio = [total[n][0:rows] / total[n][rows : 2 * rows] for n in range(2 * REACH + 1)]
    coarse_ref[...] = ratio[REACH]
    coarse = jnp.concatenate([ratio[0][1:2]] + ratio[1:-1] + [ratio[-1][0:1]], axis=0)

    lane8 = iota((deep, cols), 1)
    lane_first, lane_last = lane8 >= 1, lane8 < cols - 1
    initial = None
    for ky in range(3):
        line = coarse if ky == 1 else pltpu.roll(coarse, (1 - ky) % deep, 0)
        for kx in range(3):
            if kx == 0:
                near = jnp.where(lane_first, pltpu.roll(line, 1, 1), 0.0)
            elif kx == 2:
                near = jnp.where(lane_last, pltpu.roll(line, cols - 1, 1), 0.0)
            else:
                near = line
            term = mix_buf[3 * ky + kx] * near[None]
            initial = term if initial is None else initial + term
    initial = initial.reshape(UP, UP, deep, cols)
    pull = primal_step * inverse
    constant = pull * fidelity * initial

    line = pix * rows - 3 + iota((deep, cols), 0)
    inside_last = (line >= 0) & (line < npix * rows - 1)

    def tv(step, current):
        primal, extrap, dual_x, dual_y = current
        over = [
            jnp.where(lane_last, pltpu.roll(extrap[a, 0], cols - 1, 1) - extrap[a, UP - 1], 0.0)
            for a in range(UP)
        ]
        grad_x = jnp.concatenate(
            [extrap[:, 1:] - extrap[:, :-1], jnp.stack(over)[:, None]], axis=1
        )
        under = [
            jnp.where(inside_last, pltpu.roll(extrap[0, b], deep - 1, 0) - extrap[UP - 1, b], 0.0)
            for b in range(UP)
        ]
        grad_y = jnp.concatenate(
            [extrap[1:] - extrap[:-1], jnp.stack(under)[None]], axis=0
        )
        trial_x = dual_x + grad_x
        trial_y = dual_y + grad_y
        square = jnp.maximum(trial_x * trial_x + trial_y * trial_y, 1e-30)
        shrink = jnp.minimum(1.0, tv_bound * lax.rsqrt(square))
        dual_x = trial_x * shrink
        dual_y = trial_y * shrink
        prior = [
            jnp.where(lane_first, pltpu.roll(dual_x[a, UP - 1], 1, 1), 0.0) for a in range(UP)
        ]
        left = jnp.concatenate([jnp.stack(prior)[:, None], dual_x[:, :-1]], axis=1)
        above = [pltpu.roll(dual_y[UP - 1, b], 1, 0) for b in range(UP)]
        upper = jnp.concatenate([jnp.stack(above)[None], dual_y[:-1]], axis=0)
        divergence = dual_x - left + dual_y - upper
        updated = primal * inverse + divergence * pull + constant
        return (updated, (2.0 * dual_step) * updated - dual_step * primal, dual_x, dual_y)

    zeros = jnp.zeros_like(initial)
    result = lax.fori_loop(0, TV_ITERS, tv, (initial, dual_step * initial, zeros, zeros))[0]

    shape = (fine_rows, UP * deep)
    to, fr = iota(shape, 0), iota(shape, 1)
    own = one_hot((to % UP == fr // deep) & (to // UP + 3 == fr % deep)).astype(bf16)
    pieces = []
    for b in range(UP):
        high, low = split(result[:, b].reshape(UP * deep, cols))
        pieces.append(jnp.concatenate([dot(own, high), dot(own, low)], axis=0).astype(bf16))
    redo = one_hot((oo % UP == ii // wide) & (oo // UP == ii % wide)).astype(bf16)
    for j in range(blocks):
        packed = jnp.concatenate([v[:, j * wide : (j + 1) * wide] for v in pieces], axis=1)
        both = dot(packed, redo)
        out_ref[:, j * block : (j + 1) * block] = both[0:fine_rows] + both[fine_rows:]

    for k in (-1, 1):

        @pl.when(exists(k))
        def _():
            rows_copy(k).wait_send()

    for k, dc in partners:

        @pl.when(exists(k))
        def _():
            part_copy(k, dc).wait_send()


def local(
    left_image, right_image, feat_weight, first_weight, first_bias,
    second_weight, second_bias, head_weight, mask_weight, confidence,
):
    npix, ndisp = lax.axis_size("pix"), lax.axis_size("disp")
    fine_rows, fine_cols = left_image.shape
    rows, cols = fine_rows // UP, fine_cols // UP
    ch = feat_weight.shape[1]
    planes = DSP // ndisp
    assert fine_rows == TV_ITERS and rows == 2
    vmem = pl.BlockSpec(memory_space=pltpu.VMEM)
    args = (
        left_image, right_image, feat_weight, first_weight, first_bias[None],
        second_weight, second_bias[None], head_weight[None], mask_weight, confidence,
    )
    return pl.pallas_call(
        functools.partial(kernel, npix, ndisp),
        out_shape=(
            jax.ShapeDtypeStruct((rows, cols), f32),
            jax.ShapeDtypeStruct((fine_rows, fine_cols), f32),
        ),
        in_specs=[pl.BlockSpec(memory_space=pltpu.HBM)] * 10,
        out_specs=(vmem, vmem),
        scratch_shapes=[pltpu.VMEM(arg.shape, arg.dtype) for arg in args]
        + [
            pltpu.SemaphoreType.DMA((len(args),)),
            pltpu.VMEM((3 * rows * ch, cols), bf16),
            pltpu.VMEM((3, 2 * rows * ch + UP * fine_rows, cols), bf16),
            pltpu.VMEM((2 * REACH + 1, ndisp, 8, cols), f32),
            pltpu.VMEM((16 * ch, 16 * ch), f32),
            pltpu.VMEM((2, 12 * ch, 16 * ch), bf16),
            pltpu.VMEM((3, 4 * ch, cols), f32),
            pltpu.VMEM((2, 3 * rows * ch, cols), f32),
            pltpu.VMEM((planes + 2, 4 * ch, cols), bf16),
            pltpu.VMEM((planes // 2, 2 * rows, cols), f32),
            pltpu.VMEM((9, UP * UP, 8, cols), f32),
            pltpu.SemaphoreType.DMA((3,)),
            pltpu.SemaphoreType.DMA((3,)),
            pltpu.SemaphoreType.DMA((2 * REACH + 1, ndisp)),
            pltpu.SemaphoreType.DMA((2 * REACH + 1, ndisp)),
        ],
        compiler_params=pltpu.CompilerParams(
            collective_id=0, has_side_effects=True, vmem_limit_bytes=40 * 1024 * 1024
        ),
    )(*[pltpu.with_memory_space_constraint(arg, pltpu.HBM) for arg in args])


def solution(mesh):
    placed = (
        P(("grp", "pix"), None),
        P(("grp", "pix"), None),
        P(),
        P(),
        P(),
        P(),
        P(),
        P(),
        P(),
        P(("grp", "pix"), None),
    )
    return jax.shard_map(
        local,
        mesh=mesh,
        in_specs=placed,
        out_specs=(P(("grp", "pix"), None), P(("grp", "pix"), None)),
        check_vma=False,
    )
```

```python
import functools

import jax
import jax.numpy as jnp
from jax import lax
from jax.experimental import pallas as pl
from jax.experimental.pallas import tpu as pltpu
from jax.sharding import PartitionSpec as P

DSP = 128
UP = 4
TV_ITERS = 8
REACH = 2

dual_step = 0.175
primal_step = 0.7
tv_bound = 0.3
cost_scale = 8.0
mask_scale = 3.0
highest_prec = lax.Precision.HIGHEST
f32 = jnp.float32
bf16 = jnp.bfloat16
LANES = 128
CHUNK1 = 11
CHUNK2 = 8


def iota(shape, dim):
    return lax.broadcasted_iota(jnp.int32, shape, dim)


def one_hot(cond):
    return jnp.where(cond, 1.0, 0.0)


def dot(a, b, dims=((1,), (0,)), precision=None):
    return lax.dot_general(a, b, (dims, ((), ())), precision=precision, preferred_element_type=f32)


def column(row, groups):
    ch = row.shape[1]
    shape = (groups * ch, ch)
    return jnp.sum(
        jnp.where(iota(shape, 0) % ch == iota(shape, 1), jnp.broadcast_to(row, shape), 0.0),
        axis=1,
        keepdims=True,
    )


def split(value):
    high = value.astype(bf16)
    return high, (value - high.astype(f32)).astype(bf16)


def kernel(
    npix, ndisp,
    left_hbm, right_hbm, featw_hbm, w1_hbm, b1_hbm, w2_hbm, b2_hbm, head_hbm, mask_hbm, conf_hbm,
    coarse_ref, out_ref,
    left_ref, right_ref, featw_ref, w1_ref, b1_ref, w2_ref, b2_ref, head_ref, mask_ref, conf_ref,
    load_sem,
    keep_buf, rows_buf, part_buf, wt_buf, wmat_buf, col_buf, lr_buf, hid_buf, score_buf, mix_buf, big_buf,
    rows_send, rows_recv, part_send, part_recv,
):
    fine_rows, fine_cols = left_ref.shape
    rows = fine_rows // UP
    cols = fine_cols // UP
    ch = featw_ref.shape[1]
    planes = DSP // ndisp
    pix = lax.axis_index("pix")
    disp = lax.axis_index("disp")
    start = disp * planes

    def target(k, dc):
        return {"pix": pix + k, "disp": lax.rem(disp + dc, ndisp)}

    def exists(k):
        return (pix + k >= 0) & (pix + k < npix)

    loads = [
        pltpu.make_async_copy(src, dst, load_sem.at[n])
        for n, (src, dst) in enumerate(
            (
                (left_hbm, left_ref),
                (right_hbm, right_ref),
                (conf_hbm, conf_ref),
                (featw_hbm, featw_ref),
                (w1_hbm, w1_ref),
                (w2_hbm, w2_ref),
                (b1_hbm, b1_ref),
                (b2_hbm, b2_ref),
                (head_hbm, head_ref),
                (mask_hbm, mask_ref),
            )
        )
    ]
    for load in loads:
        load.start()

    offsets = [k for k in range(-REACH, REACH + 1)]
    barrier = pltpu.get_barrier_semaphore()
    expected = jnp.int32(0)
    for k in offsets:
        for dc in range(ndisp):
            if k == 0 and dc == 0:
                continue

            @pl.when(exists(k))
            def _():
                pl.semaphore_signal(
                    barrier, inc=1, device_id=target(k, dc), device_id_type=pl.DeviceIdType.MESH
                )

            expected = expected + jnp.where(exists(k), 1, 0)

    block = UP * (cols // UP)
    wide = block // UP
    ii, oo = iota((block, block), 0), iota((block, block), 1)
    undo = one_hot((ii % UP == oo // wide) & (ii // UP == oo % wide)).astype(bf16)
    for load in loads[:4]:
        load.wait()
    stacked = jnp.concatenate(
        [
            (left_ref[...] - 128).astype(f32) / 64.0,
            (right_ref[...] - 128).astype(f32) / 64.0,
            conf_ref[...],
            jnp.zeros((fine_rows, fine_cols), f32),
        ],
        axis=0,
    ).astype(bf16)
    tall = stacked.shape[0]
    blocks = fine_cols // block
    res = dot(
        jnp.concatenate([stacked[:, j * block : (j + 1) * block] for j in range(blocks)], axis=0),
        undo,
    )
    by_b = [
        jnp.concatenate(
            [res[j * tall : (j + 1) * tall, b * wide : (b + 1) * wide] for j in range(blocks)],
            axis=1,
        )
        for b in range(UP)
    ]
    patch_left, patch_right, conf_rows = [
        jnp.concatenate([v[n * fine_rows : (n + 1) * fine_rows] for v in by_b], axis=0)
        for n in range(3)
    ]
    patch_rows = UP * fine_rows
    pp, qq = iota((UP * UP, patch_rows), 0), iota((UP * UP, patch_rows), 1)
    pick = one_hot(pp == UP * (qq % UP) + qq // fine_rows)
    spread = dot(featw_ref[...], pick, ((0,), (0,)), highest_prec)
    spread = jnp.concatenate([spread] * rows, axis=0)
    rr, qq = iota(spread.shape, 0), iota(spread.shape, 1)
    spread = jnp.where(rr // ch == (qq % fine_rows) // UP, spread, 0.0)
    frows = rows * ch
    rows_buf[1, 0:frows, :] = dot(spread, patch_left, precision=highest_prec).astype(bf16)
    rows_buf[1, frows : 2 * frows, :] = dot(spread, patch_right, precision=highest_prec).astype(bf16)
    rows_buf[1, 2 * frows : 2 * frows + patch_rows, :] = conf_rows.astype(bf16)

    pl.semaphore_wait(barrier, expected)

    def rows_copy(k):
        return pltpu.make_async_remote_copy(
            src_ref=rows_buf.at[1],
            dst_ref=rows_buf.at[1 - k],
            send_sem=rows_send.at[1 + k],
            recv_sem=rows_recv.at[1 - k],
            device_id=target(k, 0),
            device_id_type=pl.DeviceIdType.MESH,
        )

    for k in (-1, 1):

        @pl.when(exists(k))
        def _():
            rows_copy(k).start()

        @pl.when(jnp.logical_not(exists(k)))
        def _():
            rows_buf[1 + k] = jnp.zeros(rows_buf.shape[1:], bf16)

    for load in loads[4:]:
        load.wait()

    for n, w_ref in enumerate((w1_ref, w2_ref)):
        wt_buf[...] = jnp.zeros_like(wt_buf)
        for kd in range(3):
            for ky in range(3):
                for kx in range(3):
                    tap = w_ref[kd, ky, kx].astype(f32)
                    for pd in range(2):
                        for py in range(2):
                            row = ((kd + pd) * 4 + ky + py) * ch
                            col = (kx * 4 + pd * 2 + py) * ch
                            wt_buf[row : row + ch, col : col + ch] = tap
        wmat_buf[n] = wt_buf[...].T[: 12 * ch].astype(bf16)
    group = 4 * ch
    for n, ref in enumerate((b1_ref, b2_ref, head_ref)):
        col_buf[n] = jnp.broadcast_to(column(ref[...], 4), (group, cols))

    deep = 8
    taps = mask_ref.shape[1]
    cc, qq = iota((ch, deep * ch), 0), iota((ch, deep * ch), 1)
    tiled = dot(mask_ref[...], one_hot(cc == qq % ch), ((0,), (0,)), highest_prec)
    shape = (taps, deep, deep * ch)
    big = jnp.where(
        iota(shape, 1) == iota(shape, 2) // ch, jnp.broadcast_to(tiled[:, None, :], shape), 0.0
    ).reshape(taps * deep, deep * ch)
    big_buf[...] = jnp.concatenate(split(big), axis=1)

    step1 = 2 * CHUNK1
    for n in range(1, step1 + 1):
        keep_buf[n] = one_hot(iota(keep_buf.shape[1:], 1) >= n).astype(bf16)

    def rows_wait(k):
        return pltpu.make_async_remote_copy(
            src_ref=rows_buf.at[1],
            dst_ref=rows_buf.at[1 + k],
            send_sem=rows_send.at[1 + k],
            recv_sem=rows_recv.at[1 + k],
            device_id=target(k, 0),
            device_id_type=pl.DeviceIdType.MESH,
        )

    for k in (-1, 1):

        @pl.when(exists(k))
        def _():
            rows_wait(k).wait_recv()

    for slot in range(3):
        for side in range(2):
            lr_buf[side, slot * frows : (slot + 1) * frows, :] = rows_buf[
                slot, side * frows : (side + 1) * frows, :
            ].astype(f32)

    lane = iota((group, LANES), 1)
    not_first = lane >= 1
    not_last = lane < LANES - 1

    def conv(weights, values):
        acc = dot(weights, values)
        moved_right, moved_left = {}, {}
        parts = []
        for n in range(cols // LANES):
            at = slice(n * LANES, (n + 1) * LANES)
            moved_right[n] = pltpu.roll(acc[0:group, at], 1, 1)
            moved_left[n] = pltpu.roll(acc[2 * group :, at], LANES - 1, 1)
        for n in range(cols // LANES):
            at = slice(n * LANES, (n + 1) * LANES)
            before = jnp.where(not_first, moved_right[n], moved_right.get(n - 1, 0.0))
            after = jnp.where(not_last, moved_left[n], moved_left.get(n + 1, 0.0))
            parts.append(acc[group : 2 * group, at] + before + after)
        return jnp.concatenate(parts, axis=1)

    def volume(plane):
        shift = lax.rem(plane + cols, cols)
        moved = pltpu.roll(lr_buf[1], shift, 1)
        keep = (iota(moved.shape, 1) >= plane) & (plane >= 0) & (plane < DSP)
        return jnp.where(keep, moved * lr_buf[0], 0.0).astype(bf16)

    vrows = 4 * ch
    half = 2 * ch

    left_rows = lr_buf[0].astype(bf16)
    def shifted(value, n, inside=None):
        if n == 0:
            return value if inside is None else value * inside
        keep = keep_buf[n] if inside is None else keep_buf[n] * inside
        rolled = pltpu.roll(value, n, 1)
        return (rolled.reshape(-1, ch, cols) * keep[None]).reshape(rolled.shape)

    def first(c, carry):
        base = c * step1
        held, origin = list(carry[:2]), carry[2]
        for j in range(CHUNK1):
            held = held[-2:]
            for n in (2 * j, 2 * j + 1):
                inside = None
                if n >= step1 - 2:
                    inside = (start + base + n < DSP).astype(f32).astype(bf16)
                held.append(shifted(origin, n, inside) * left_rows)
            for rb in range(2):
                values = jnp.concatenate([v[rb * half : rb * half + vrows] for v in held], axis=0)
                got = jnp.maximum(conv(wmat_buf[0], values) + col_buf[0], 0.0).astype(bf16)
                for pd in range(2):
                    hid_buf[base + 2 * j + pd, rb * half : (rb + 1) * half, :] = got[
                        pd * half : (pd + 1) * half
                    ]
        return (held[-2], held[-1], shifted(origin, step1))

    opening = jnp.where(
        iota(lr_buf.shape[1:], 1) >= start, pltpu.roll(lr_buf[1], start, 1), 0.0
    ).astype(bf16)
    lax.fori_loop(
        0,
        (planes // 2 + 1) // CHUNK1,
        first,
        (volume(start - 2), volume(start - 1), opening),
    )

    @pl.when(pix == 0)
    def _():
        hid_buf[:, 0:ch, :] = jnp.zeros((planes + 2, ch, cols), bf16)

    @pl.when(pix == npix - 1)
    def _():
        hid_buf[:, 3 * ch : 4 * ch, :] = jnp.zeros((planes + 2, ch, cols), bf16)

    @pl.when(disp == 0)
    def _():
        hid_buf[0] = jnp.zeros((4 * ch, cols), bf16)

    @pl.when(disp == ndisp - 1)
    def _():
        hid_buf[planes + 1] = jnp.zeros((4 * ch, cols), bf16)

    def second(c, carry):
        base = c * CHUNK2
        for j in range(CHUNK2):
            values = hid_buf[pl.ds(2 * (base + j), 4)].reshape(4 * vrows, cols)
            got = jnp.maximum(conv(wmat_buf[1], values) + col_buf[1], 0.0) * col_buf[2]
            score_buf[base + j] = jnp.sum(got.reshape(4, ch, cols), axis=1)
        return carry

    lax.fori_loop(0, planes // 2 // CHUNK2, second, 0)

    expo = jnp.exp(-cost_scale * jnp.tanh(score_buf[...]))
    shape = expo.shape
    plane = start + 2 * iota(shape, 0) + iota(shape, 1) // rows
    weight4 = jnp.sum(expo, axis=0)
    plane4 = jnp.sum(expo * (plane.astype(f32) / DSP), axis=0)
    mine = jnp.concatenate(
        [plane4[0:rows] + plane4[rows:], weight4[0:rows] + weight4[rows:], jnp.ones((4, cols), f32)],
        axis=0,
    )
    part_buf[REACH, disp] = mine

    def part_copy(k, dc):
        return pltpu.make_async_remote_copy(
            src_ref=part_buf.at[REACH, disp],
            dst_ref=part_buf.at[REACH - k, disp],
            send_sem=part_send.at[REACH + k, dc],
            recv_sem=part_recv.at[REACH - k, disp],
            device_id=target(k, dc),
            device_id_type=pl.DeviceIdType.MESH,
        )

    def part_wait(k, dc):
        core = lax.rem(disp + dc, ndisp)
        return pltpu.make_async_remote_copy(
            src_ref=part_buf.at[REACH, disp],
            dst_ref=part_buf.at[REACH + k, core],
            send_sem=part_send.at[REACH + k, dc],
            recv_sem=part_recv.at[REACH + k, core],
            device_id=target(k, dc),
            device_id_type=pl.DeviceIdType.MESH,
        )

    partners = [(k, dc) for k in (2, -2, 1, -1, 0) for dc in range(ndisp) if (k, dc) != (0, 0)]
    for k, dc in partners:

        @pl.when(exists(k))
        def _():
            part_copy(k, dc).start()

    for k in (-2, -1, 1, 2):

        @pl.when(jnp.logical_not(exists(k)))
        def _():
            for core in range(ndisp):
                part_buf[REACH + k, core] = jnp.where(iota((8, cols), 0) < rows, 0.0, 1.0)

    none = jnp.zeros((ch, cols), bf16)
    lines = jnp.concatenate(
        [none] + [rows_buf[slot, 0:frows, :] for slot in range(3)] + [none], axis=0
    )
    logits = dot(big_buf[...], jnp.concatenate([lines, lines], axis=0))
    expo = jnp.exp(mask_scale * jnp.tanh(logits)).reshape(9, UP * UP, deep, cols)
    mix_buf[...] = expo * (1.0 / jnp.sum(expo, axis=0))[None]

    conf_all = jnp.concatenate(
        [rows_buf[slot, 2 * frows : 2 * frows + patch_rows, :] for slot in range(3)], axis=0
    )
    shape = (UP * UP * deep, 3 * patch_rows)
    to, fr = iota(shape, 0), iota(shape, 1)
    to_a, to_b, to_s = to // (UP * deep), (to // deep) % UP, to % deep
    fr_slot, fr_b, fr_r, fr_a = fr // patch_rows, (fr // fine_rows) % UP, (fr // UP) % rows, fr % UP
    place = one_hot((to_a == fr_a) & (to_b == fr_b) & (to_s - 1 == fr_slot * rows + fr_r))
    fidelity = dot(place.astype(bf16), conf_all).reshape(UP, UP, deep, cols)
    inverse = 1.0 / (1.0 + primal_step * fidelity)

    for k, dc in partners:

        @pl.when(exists(k))
        def _():
            part_wait(k, dc).wait_recv()

    total = part_buf[:, 0]
    for core in range(1, ndisp):
        total = total + part_buf[:, core]
    ratio = [total[n][0:rows] / total[n][rows : 2 * rows] for n in range(2 * REACH + 1)]
    coarse_ref[...] = ratio[REACH]
    coarse = jnp.concatenate([ratio[0][1:2]] + ratio[1:-1] + [ratio[-1][0:1]], axis=0)

    lane8 = iota((deep, cols), 1)
    lane_first, lane_last = lane8 >= 1, lane8 < cols - 1
    initial = None
    for ky in range(3):
        line = coarse if ky == 1 else pltpu.roll(coarse, (1 - ky) % deep, 0)
        for kx in range(3):
            if kx == 0:
                near = jnp.where(lane_first, pltpu.roll(line, 1, 1), 0.0)
            elif kx == 2:
                near = jnp.where(lane_last, pltpu.roll(line, cols - 1, 1), 0.0)
            else:
                near = line
            term = mix_buf[3 * ky + kx] * near[None]
            initial = term if initial is None else initial + term
    initial = initial.reshape(UP, UP, deep, cols)
    pull = primal_step * inverse
    constant = pull * fidelity * initial

    line = pix * rows - 3 + iota((deep, cols), 0)
    inside_last = (line >= 0) & (line < npix * rows - 1)

    def tv(step, current):
        primal, extrap, dual_x, dual_y = current
        over = [
            jnp.where(lane_last, pltpu.roll(extrap[a, 0], cols - 1, 1) - extrap[a, UP - 1], 0.0)
            for a in range(UP)
        ]
        grad_x = jnp.concatenate(
            [extrap[:, 1:] - extrap[:, :-1], jnp.stack(over)[:, None]], axis=1
        )
        under = [
            jnp.where(inside_last, pltpu.roll(extrap[0, b], deep - 1, 0) - extrap[UP - 1, b], 0.0)
            for b in range(UP)
        ]
        grad_y = jnp.concatenate(
            [extrap[1:] - extrap[:-1], jnp.stack(under)[None]], axis=0
        )
        trial_x = dual_x + grad_x
        trial_y = dual_y + grad_y
        square = jnp.maximum(trial_x * trial_x + trial_y * trial_y, 1e-30)
        shrink = jnp.minimum(1.0, tv_bound * lax.rsqrt(square))
        dual_x = trial_x * shrink
        dual_y = trial_y * shrink
        prior = [
            jnp.where(lane_first, pltpu.roll(dual_x[a, UP - 1], 1, 1), 0.0) for a in range(UP)
        ]
        left = jnp.concatenate([jnp.stack(prior)[:, None], dual_x[:, :-1]], axis=1)
        above = [pltpu.roll(dual_y[UP - 1, b], 1, 0) for b in range(UP)]
        upper = jnp.concatenate([jnp.stack(above)[None], dual_y[:-1]], axis=0)
        divergence = dual_x - left + dual_y - upper
        updated = primal * inverse + divergence * pull + constant
        return (updated, (2.0 * dual_step) * updated - dual_step * primal, dual_x, dual_y)

    zeros = jnp.zeros_like(initial)
    result = lax.fori_loop(
        0, TV_ITERS, tv, (initial, dual_step * initial, zeros, zeros), unroll=4
    )[0]

    shape = (fine_rows, UP * deep)
    to, fr = iota(shape, 0), iota(shape, 1)
    own = one_hot((to % UP == fr // deep) & (to // UP + 3 == fr % deep)).astype(bf16)
    pieces = []
    for b in range(UP):
        high, low = split(result[:, b].reshape(UP * deep, cols))
        pieces.append(jnp.concatenate([dot(own, high), dot(own, low)], axis=0).astype(bf16))
    redo = one_hot((oo % UP == ii // wide) & (oo // UP == ii % wide)).astype(bf16)
    for j in range(blocks):
        packed = jnp.concatenate([v[:, j * wide : (j + 1) * wide] for v in pieces], axis=1)
        both = dot(packed, redo)
        out_ref[:, j * block : (j + 1) * block] = both[0:fine_rows] + both[fine_rows:]

    for k in (-1, 1):

        @pl.when(exists(k))
        def _():
            rows_copy(k).wait_send()

    for k, dc in partners:

        @pl.when(exists(k))
        def _():
            part_copy(k, dc).wait_send()


def local(
    left_image, right_image, feat_weight, first_weight, first_bias,
    second_weight, second_bias, head_weight, mask_weight, confidence,
):
    npix, ndisp = lax.axis_size("pix"), lax.axis_size("disp")
    fine_rows, fine_cols = left_image.shape
    rows, cols = fine_rows // UP, fine_cols // UP
    ch = feat_weight.shape[1]
    planes = DSP // ndisp
    assert fine_rows == TV_ITERS and rows == 2
    vmem = pl.BlockSpec(memory_space=pltpu.VMEM)
    args = (
        left_image, right_image, feat_weight, first_weight, first_bias[None],
        second_weight, second_bias[None], head_weight[None], mask_weight, confidence,
    )
    return pl.pallas_call(
        functools.partial(kernel, npix, ndisp),
        out_shape=(
            jax.ShapeDtypeStruct((rows, cols), f32),
            jax.ShapeDtypeStruct((fine_rows, fine_cols), f32),
        ),
        in_specs=[pl.BlockSpec(memory_space=pltpu.HBM)] * 10,
        out_specs=(vmem, vmem),
        scratch_shapes=[pltpu.VMEM(arg.shape, arg.dtype) for arg in args]
        + [
            pltpu.SemaphoreType.DMA((len(args),)),
            pltpu.VMEM((2 * CHUNK1 + 1, ch, cols), bf16),
            pltpu.VMEM((3, 2 * rows * ch + UP * fine_rows, cols), bf16),
            pltpu.VMEM((2 * REACH + 1, ndisp, 8, cols), f32),
            pltpu.VMEM((16 * ch, 16 * ch), f32),
            pltpu.VMEM((2, 12 * ch, 16 * ch), bf16),
            pltpu.VMEM((3, 4 * ch, cols), f32),
            pltpu.VMEM((2, 3 * rows * ch, cols), f32),
            pltpu.VMEM((planes + 2, 4 * ch, cols), bf16),
            pltpu.VMEM((planes // 2, 2 * rows, cols), f32),
            pltpu.VMEM((9, UP * UP, 8, cols), f32),
            pltpu.VMEM((mask_weight.shape[1] * 8, 2 * 8 * ch), bf16),
            pltpu.SemaphoreType.DMA((3,)),
            pltpu.SemaphoreType.DMA((3,)),
            pltpu.SemaphoreType.DMA((2 * REACH + 1, ndisp)),
            pltpu.SemaphoreType.DMA((2 * REACH + 1, ndisp)),
        ],
        compiler_params=pltpu.CompilerParams(
            collective_id=0, has_side_effects=True, vmem_limit_bytes=40 * 1024 * 1024
        ),
    )(*[pltpu.with_memory_space_constraint(arg, pltpu.HBM) for arg in args])


def solution(mesh):
    placed = (
        P(("grp", "pix"), None),
        P(("grp", "pix"), None),
        P(),
        P(),
        P(),
        P(),
        P(),
        P(),
        P(),
        P(("grp", "pix"), None),
    )
    return jax.shard_map(
        local,
        mesh=mesh,
        in_specs=placed,
        out_specs=(P(("grp", "pix"), None), P(("grp", "pix"), None)),
        check_vma=False,
    )
```

```python
import functools

import jax
import jax.numpy as jnp
from jax import lax
from jax.experimental import pallas as pl
from jax.experimental.pallas import tpu as pltpu
from jax.sharding import PartitionSpec as P

DSP = 128
UP = 4
TV_ITERS = 8
REACH = 2

dual_step = 0.175
primal_step = 0.7
tv_bound = 0.3
cost_scale = 8.0
mask_scale = 3.0
highest_prec = lax.Precision.HIGHEST
f32 = jnp.float32
bf16 = jnp.bfloat16
LANES = 128
CHUNK1 = 11


def iota(shape, dim):
    return lax.broadcasted_iota(jnp.int32, shape, dim)


def one_hot(cond):
    return jnp.where(cond, 1.0, 0.0)


def dot(a, b, dims=((1,), (0,)), precision=None):
    return lax.dot_general(a, b, (dims, ((), ())), precision=precision, preferred_element_type=f32)


def column(row, groups):
    ch = row.shape[1]
    shape = (groups * ch, ch)
    return jnp.sum(
        jnp.where(iota(shape, 0) % ch == iota(shape, 1), jnp.broadcast_to(row, shape), 0.0),
        axis=1,
        keepdims=True,
    )


def split(value):
    high = value.astype(bf16)
    return high, (value - high.astype(f32)).astype(bf16)


def kernel(
    npix, ndisp,
    left_hbm, right_hbm, featw_hbm, w1_hbm, b1_hbm, w2_hbm, b2_hbm, head_hbm, mask_hbm, conf_hbm,
    coarse_ref, out_ref,
    left_ref, right_ref, featw_ref, w1_ref, b1_ref, w2_ref, b2_ref, head_ref, mask_ref, conf_ref,
    load_sem,
    keep_buf, rows_buf, part_buf, wt_buf, wmat_buf, col_buf, bias_buf, lr_buf, score_buf, mix_buf, big_buf,
    rows_send, rows_recv, part_send, part_recv,
):
    fine_rows, fine_cols = left_ref.shape
    rows = fine_rows // UP
    cols = fine_cols // UP
    ch = featw_ref.shape[1]
    planes = DSP // ndisp
    pix = lax.axis_index("pix")
    disp = lax.axis_index("disp")
    start = disp * planes

    def target(k, dc):
        return {"pix": pix + k, "disp": lax.rem(disp + dc, ndisp)}

    def exists(k):
        return (pix + k >= 0) & (pix + k < npix)

    loads = [
        pltpu.make_async_copy(src, dst, load_sem.at[n])
        for n, (src, dst) in enumerate(
            (
                (left_hbm, left_ref),
                (right_hbm, right_ref),
                (conf_hbm, conf_ref),
                (featw_hbm, featw_ref),
                (w1_hbm, w1_ref),
                (w2_hbm, w2_ref),
                (b1_hbm, b1_ref),
                (b2_hbm, b2_ref),
                (head_hbm, head_ref),
                (mask_hbm, mask_ref),
            )
        )
    ]
    for load in loads:
        load.start()

    offsets = [k for k in range(-REACH, REACH + 1)]
    barrier = pltpu.get_barrier_semaphore()
    expected = jnp.int32(0)
    for k in offsets:
        for dc in range(ndisp):
            if k == 0 and dc == 0:
                continue

            @pl.when(exists(k))
            def _():
                pl.semaphore_signal(
                    barrier, inc=1, device_id=target(k, dc), device_id_type=pl.DeviceIdType.MESH
                )

            expected = expected + jnp.where(exists(k), 1, 0)

    block = UP * (cols // UP)
    wide = block // UP
    ii, oo = iota((block, block), 0), iota((block, block), 1)
    undo = one_hot((ii % UP == oo // wide) & (ii // UP == oo % wide)).astype(bf16)
    for load in loads[:4]:
        load.wait()
    stacked = jnp.concatenate(
        [
            (left_ref[...] - 128).astype(f32) / 64.0,
            (right_ref[...] - 128).astype(f32) / 64.0,
            conf_ref[...],
            jnp.zeros((fine_rows, fine_cols), f32),
        ],
        axis=0,
    ).astype(bf16)
    tall = stacked.shape[0]
    blocks = fine_cols // block
    res = dot(
        jnp.concatenate([stacked[:, j * block : (j + 1) * block] for j in range(blocks)], axis=0),
        undo,
    )
    by_b = [
        jnp.concatenate(
            [res[j * tall : (j + 1) * tall, b * wide : (b + 1) * wide] for j in range(blocks)],
            axis=1,
        )
        for b in range(UP)
    ]
    patch_left, patch_right, conf_rows = [
        jnp.concatenate([v[n * fine_rows : (n + 1) * fine_rows] for v in by_b], axis=0)
        for n in range(3)
    ]
    patch_rows = UP * fine_rows
    pp, qq = iota((UP * UP, patch_rows), 0), iota((UP * UP, patch_rows), 1)
    pick = one_hot(pp == UP * (qq % UP) + qq // fine_rows)
    spread = dot(featw_ref[...], pick, ((0,), (0,)), highest_prec)
    spread = jnp.concatenate([spread] * rows, axis=0)
    rr, qq = iota(spread.shape, 0), iota(spread.shape, 1)
    spread = jnp.where(rr // ch == (qq % fine_rows) // UP, spread, 0.0)
    frows = rows * ch
    rows_buf[1, 0:frows, :] = dot(spread, patch_left, precision=highest_prec).astype(bf16)
    rows_buf[1, frows : 2 * frows, :] = dot(spread, patch_right, precision=highest_prec).astype(bf16)
    rows_buf[1, 2 * frows : 2 * frows + patch_rows, :] = conf_rows.astype(bf16)

    pl.semaphore_wait(barrier, expected)

    def rows_copy(k):
        return pltpu.make_async_remote_copy(
            src_ref=rows_buf.at[1],
            dst_ref=rows_buf.at[1 - k],
            send_sem=rows_send.at[1 + k],
            recv_sem=rows_recv.at[1 - k],
            device_id=target(k, 0),
            device_id_type=pl.DeviceIdType.MESH,
        )

    for k in (-1, 1):

        @pl.when(exists(k))
        def _():
            rows_copy(k).start()

        @pl.when(jnp.logical_not(exists(k)))
        def _():
            rows_buf[1 + k] = jnp.zeros(rows_buf.shape[1:], bf16)

    for load in loads[4:]:
        load.wait()

    for n, w_ref in enumerate((w1_ref, w2_ref)):
        wt_buf[...] = jnp.zeros_like(wt_buf)
        for kd in range(3):
            for ky in range(3):
                for kx in range(3):
                    tap = w_ref[kd, ky, kx].astype(f32)
                    for pd in range(2):
                        for py in range(2):
                            row = ((kd + pd) * 4 + ky + py) * ch
                            col = (kx * 4 + pd * 2 + py) * ch
                            wt_buf[row : row + ch, col : col + ch] = tap
        wmat_buf[n] = wt_buf[...].T[: 12 * ch].astype(bf16)
    group = 4 * ch
    for n, ref in enumerate((b2_ref, head_ref)):
        col_buf[n] = jnp.broadcast_to(column(ref[...], 4), (group, cols))
    shift1 = jnp.broadcast_to(column(b1_ref[...], 4), (group, cols))
    place_d = iota((group, cols), 0) // (2 * ch)
    place_y = iota((group, cols), 0) // ch % 2
    no_plane = [
        (place_d == 0) & (disp == 0),
        (place_d == 1) & (disp == ndisp - 1),
    ]
    no_row = [(place_y == 0) & (pix == 0), (place_y == 1) & (pix == npix - 1)]
    for rb in range(2):
        for which in range(4):
            value = jnp.where(no_row[rb], -1e30, shift1)
            for n in range(2):
                if which & (n + 1):
                    value = jnp.where(no_plane[n], -1e30, value)
            bias_buf[rb, which] = value

    deep = 8
    taps = mask_ref.shape[1]
    cc, qq = iota((ch, deep * ch), 0), iota((ch, deep * ch), 1)
    tiled = dot(mask_ref[...], one_hot(cc == qq % ch), ((0,), (0,)), highest_prec)
    shape = (taps, deep, deep * ch)
    big = jnp.where(
        iota(shape, 1) == iota(shape, 2) // ch, jnp.broadcast_to(tiled[:, None, :], shape), 0.0
    ).reshape(taps * deep, deep * ch)
    big_buf[...] = jnp.concatenate(split(big), axis=1)

    step1 = 2 * CHUNK1
    for n in range(1, step1 + 1):
        keep_buf[n] = one_hot(iota(keep_buf.shape[1:], 1) >= n).astype(bf16)

    def rows_wait(k):
        return pltpu.make_async_remote_copy(
            src_ref=rows_buf.at[1],
            dst_ref=rows_buf.at[1 + k],
            send_sem=rows_send.at[1 + k],
            recv_sem=rows_recv.at[1 + k],
            device_id=target(k, 0),
            device_id_type=pl.DeviceIdType.MESH,
        )

    for k in (-1, 1):

        @pl.when(exists(k))
        def _():
            rows_wait(k).wait_recv()

    for slot in range(3):
        for side in range(2):
            lr_buf[side, slot * frows : (slot + 1) * frows, :] = rows_buf[
                slot, side * frows : (side + 1) * frows, :
            ].astype(f32)

    lane = iota((group, LANES), 1)
    not_first = lane >= 1
    not_last = lane < LANES - 1

    def conv(weights, values):
        acc = dot(weights, values)
        moved_right, moved_left = {}, {}
        parts = []
        for n in range(cols // LANES):
            at = slice(n * LANES, (n + 1) * LANES)
            moved_right[n] = pltpu.roll(acc[0:group, at], 1, 1)
            moved_left[n] = pltpu.roll(acc[2 * group :, at], LANES - 1, 1)
        for n in range(cols // LANES):
            at = slice(n * LANES, (n + 1) * LANES)
            before = jnp.where(not_first, moved_right[n], moved_right.get(n - 1, 0.0))
            after = jnp.where(not_last, moved_left[n], moved_left.get(n + 1, 0.0))
            parts.append(acc[group : 2 * group, at] + before + after)
        return jnp.concatenate(parts, axis=1)

    def volume(plane):
        shift = lax.rem(plane + cols, cols)
        moved = pltpu.roll(lr_buf[1], shift, 1)
        keep = (iota(moved.shape, 1) >= plane) & (plane >= 0) & (plane < DSP)
        return jnp.where(keep, moved * lr_buf[0], 0.0).astype(bf16)

    vrows = 4 * ch
    half = 2 * ch

    left_rows = lr_buf[0].astype(bf16)
    def shifted(value, n, inside=None):
        if n == 0:
            return value if inside is None else value * inside
        keep = keep_buf[n] if inside is None else keep_buf[n] * inside
        rolled = pltpu.roll(value, n, 1)
        return (rolled.reshape(-1, ch, cols) * keep[None]).reshape(rolled.shape)

    count = planes // 2 + 1

    def step(c, carry):
        base = c * step1
        held, kept, origin = list(carry[:2]), list(carry[2:4]), carry[4]
        for j in range(CHUNK1):
            held = held[-2:]
            for n in (2 * j, 2 * j + 1):
                inside = None
                if n >= step1 - 2:
                    inside = (start + base + n < DSP).astype(f32).astype(bf16)
                held.append(shifted(origin, n, inside) * left_rows)
            which = 0
            if j == 0:
                which = jnp.where(c == 0, 1, 0)
            if j == CHUNK1 - 1:
                which = which + jnp.where(c == count // CHUNK1 - 1, 2, 0)
            parts = []
            for rb in range(2):
                values = jnp.concatenate([v[rb * half : rb * half + vrows] for v in held], axis=0)
                parts.append(
                    jnp.maximum(conv(wmat_buf[0], values) + bias_buf[rb, which], 0.0).astype(bf16)
                )
            kept = kept[-2:] + [
                jnp.concatenate([v[pd * half : (pd + 1) * half] for v in parts], axis=0)
                for pd in range(2)
            ]
            got = jnp.maximum(conv(wmat_buf[1], jnp.concatenate(kept, axis=0)) + col_buf[0], 0.0)
            score_buf[c * CHUNK1 + j] = jnp.sum((got * col_buf[1]).reshape(4, ch, cols), axis=1)
        return (held[-2], held[-1], kept[-2], kept[-1], shifted(origin, step1))

    opening = jnp.where(
        iota(lr_buf.shape[1:], 1) >= start, pltpu.roll(lr_buf[1], start, 1), 0.0
    ).astype(bf16)
    empty = jnp.zeros((vrows, cols), bf16)
    lax.fori_loop(
        0,
        count // CHUNK1,
        step,
        (volume(start - 2), volume(start - 1), empty, empty, opening),
    )

    expo = jnp.exp(-cost_scale * jnp.tanh(score_buf[1:]))
    shape = expo.shape
    plane = start + 2 * iota(shape, 0) + iota(shape, 1) // rows
    weight4 = jnp.sum(expo, axis=0)
    plane4 = jnp.sum(expo * (plane.astype(f32) / DSP), axis=0)
    mine = jnp.concatenate(
        [plane4[0:rows] + plane4[rows:], weight4[0:rows] + weight4[rows:], jnp.ones((4, cols), f32)],
        axis=0,
    )
    part_buf[REACH, disp] = mine

    def part_copy(k, dc):
        return pltpu.make_async_remote_copy(
            src_ref=part_buf.at[REACH, disp],
            dst_ref=part_buf.at[REACH - k, disp],
            send_sem=part_send.at[REACH + k, dc],
            recv_sem=part_recv.at[REACH - k, disp],
            device_id=target(k, dc),
            device_id_type=pl.DeviceIdType.MESH,
        )

    def part_wait(k, dc):
        core = lax.rem(disp + dc, ndisp)
        return pltpu.make_async_remote_copy(
            src_ref=part_buf.at[REACH, disp],
            dst_ref=part_buf.at[REACH + k, core],
            send_sem=part_send.at[REACH + k, dc],
            recv_sem=part_recv.at[REACH + k, core],
            device_id=target(k, dc),
            device_id_type=pl.DeviceIdType.MESH,
        )

    partners = [(k, dc) for k in (2, -2, 1, -1, 0) for dc in range(ndisp) if (k, dc) != (0, 0)]
    for k, dc in partners:

        @pl.when(exists(k))
        def _():
            part_copy(k, dc).start()

    for k in (-2, -1, 1, 2):

        @pl.when(jnp.logical_not(exists(k)))
        def _():
            for core in range(ndisp):
                part_buf[REACH + k, core] = jnp.where(iota((8, cols), 0) < rows, 0.0, 1.0)

    none = jnp.zeros((ch, cols), bf16)
    lines = jnp.concatenate(
        [none] + [rows_buf[slot, 0:frows, :] for slot in range(3)] + [none], axis=0
    )
    logits = dot(big_buf[...], jnp.concatenate([lines, lines], axis=0))
    expo = jnp.exp(mask_scale * jnp.tanh(logits)).reshape(9, UP * UP, deep, cols)
    mix_buf[...] = expo * (1.0 / jnp.sum(expo, axis=0))[None]

    conf_all = jnp.concatenate(
        [rows_buf[slot, 2 * frows : 2 * frows + patch_rows, :] for slot in range(3)], axis=0
    )
    shape = (UP * UP * deep, 3 * patch_rows)
    to, fr = iota(shape, 0), iota(shape, 1)
    to_a, to_b, to_s = to // (UP * deep), (to // deep) % UP, to % deep
    fr_slot, fr_b, fr_r, fr_a = fr // patch_rows, (fr // fine_rows) % UP, (fr // UP) % rows, fr % UP
    place = one_hot((to_a == fr_a) & (to_b == fr_b) & (to_s - 1 == fr_slot * rows + fr_r))
    fidelity = dot(place.astype(bf16), conf_all).reshape(UP, UP, deep, cols)
    inverse = 1.0 / (1.0 + primal_step * fidelity)

    for k, dc in partners:

        @pl.when(exists(k))
        def _():
            part_wait(k, dc).wait_recv()

    total = part_buf[:, 0]
    for core in range(1, ndisp):
        total = total + part_buf[:, core]
    ratio = [total[n][0:rows] / total[n][rows : 2 * rows] for n in range(2 * REACH + 1)]
    coarse_ref[...] = ratio[REACH]
    coarse = jnp.concatenate([ratio[0][1:2]] + ratio[1:-1] + [ratio[-1][0:1]], axis=0)

    lane8 = iota((deep, cols), 1)
    lane_first, lane_last = lane8 >= 1, lane8 < cols - 1
    initial = None
    for ky in range(3):
        line = coarse if ky == 1 else pltpu.roll(coarse, (1 - ky) % deep, 0)
        for kx in range(3):
            if kx == 0:
                near = jnp.where(lane_first, pltpu.roll(line, 1, 1), 0.0)
            elif kx == 2:
                near = jnp.where(lane_last, pltpu.roll(line, cols - 1, 1), 0.0)
            else:
                near = line
            term = mix_buf[3 * ky + kx] * near[None]
            initial = term if initial is None else initial + term
    initial = initial.reshape(UP, UP, deep, cols)
    pull = primal_step * inverse
    constant = pull * fidelity * initial

    line = pix * rows - 3 + iota((deep, cols), 0)
    inside_last = (line >= 0) & (line < npix * rows - 1)

    def tv(step, current):
        primal, extrap, dual_x, dual_y = current
        over = [
            jnp.where(lane_last, pltpu.roll(extrap[a, 0], cols - 1, 1) - extrap[a, UP - 1], 0.0)
            for a in range(UP)
        ]
        grad_x = jnp.concatenate(
            [extrap[:, 1:] - extrap[:, :-1], jnp.stack(over)[:, None]], axis=1
        )
        under = [
            jnp.where(inside_last, pltpu.roll(extrap[0, b], deep - 1, 0) - extrap[UP - 1, b], 0.0)
            for b in range(UP)
        ]
        grad_y = jnp.concatenate(
            [extrap[1:] - extrap[:-1], jnp.stack(under)[None]], axis=0
        )
        trial_x = dual_x + grad_x
        trial_y = dual_y + grad_y
        square = jnp.maximum(trial_x * trial_x + trial_y * trial_y, 1e-30)
        shrink = jnp.minimum(1.0, tv_bound * lax.rsqrt(square))
        dual_x = trial_x * shrink
        dual_y = trial_y * shrink
        prior = [
            jnp.where(lane_first, pltpu.roll(dual_x[a, UP - 1], 1, 1), 0.0) for a in range(UP)
        ]
        left = jnp.concatenate([jnp.stack(prior)[:, None], dual_x[:, :-1]], axis=1)
        above = [pltpu.roll(dual_y[UP - 1, b], 1, 0) for b in range(UP)]
        upper = jnp.concatenate([jnp.stack(above)[None], dual_y[:-1]], axis=0)
        divergence = dual_x - left + dual_y - upper
        updated = primal * inverse + divergence * pull + constant
        return (updated, (2.0 * dual_step) * updated - dual_step * primal, dual_x, dual_y)

    zeros = jnp.zeros_like(initial)
    result = lax.fori_loop(
        0, TV_ITERS, tv, (initial, dual_step * initial, zeros, zeros), unroll=4
    )[0]

    shape = (fine_rows, UP * deep)
    to, fr = iota(shape, 0), iota(shape, 1)
    own = one_hot((to % UP == fr // deep) & (to // UP + 3 == fr % deep)).astype(bf16)
    pieces = []
    for b in range(UP):
        high, low = split(result[:, b].reshape(UP * deep, cols))
        pieces.append(jnp.concatenate([dot(own, high), dot(own, low)], axis=0).astype(bf16))
    redo = one_hot((oo % UP == ii // wide) & (oo // UP == ii % wide)).astype(bf16)
    for j in range(blocks):
        packed = jnp.concatenate([v[:, j * wide : (j + 1) * wide] for v in pieces], axis=1)
        both = dot(packed, redo)
        out_ref[:, j * block : (j + 1) * block] = both[0:fine_rows] + both[fine_rows:]

    for k in (-1, 1):

        @pl.when(exists(k))
        def _():
            rows_copy(k).wait_send()

    for k, dc in partners:

        @pl.when(exists(k))
        def _():
            part_copy(k, dc).wait_send()


def local(
    left_image, right_image, feat_weight, first_weight, first_bias,
    second_weight, second_bias, head_weight, mask_weight, confidence,
):
    npix, ndisp = lax.axis_size("pix"), lax.axis_size("disp")
    fine_rows, fine_cols = left_image.shape
    rows, cols = fine_rows // UP, fine_cols // UP
    ch = feat_weight.shape[1]
    planes = DSP // ndisp
    assert fine_rows == TV_ITERS and rows == 2
    vmem = pl.BlockSpec(memory_space=pltpu.VMEM)
    args = (
        left_image, right_image, feat_weight, first_weight, first_bias[None],
        second_weight, second_bias[None], head_weight[None], mask_weight, confidence,
    )
    return pl.pallas_call(
        functools.partial(kernel, npix, ndisp),
        out_shape=(
            jax.ShapeDtypeStruct((rows, cols), f32),
            jax.ShapeDtypeStruct((fine_rows, fine_cols), f32),
        ),
        in_specs=[pl.BlockSpec(memory_space=pltpu.HBM)] * 10,
        out_specs=(vmem, vmem),
        scratch_shapes=[pltpu.VMEM(arg.shape, arg.dtype) for arg in args]
        + [
            pltpu.SemaphoreType.DMA((len(args),)),
            pltpu.VMEM((2 * CHUNK1 + 1, ch, cols), bf16),
            pltpu.VMEM((3, 2 * rows * ch + UP * fine_rows, cols), bf16),
            pltpu.VMEM((2 * REACH + 1, ndisp, 8, cols), f32),
            pltpu.VMEM((16 * ch, 16 * ch), f32),
            pltpu.VMEM((2, 12 * ch, 16 * ch), bf16),
            pltpu.VMEM((2, 4 * ch, cols), f32),
            pltpu.VMEM((2, 4, 4 * ch, cols), f32),
            pltpu.VMEM((2, 3 * rows * ch, cols), f32),
            pltpu.VMEM((planes // 2 + 1, 2 * rows, cols), f32),
            pltpu.VMEM((9, UP * UP, 8, cols), f32),
            pltpu.VMEM((mask_weight.shape[1] * 8, 2 * 8 * ch), bf16),
            pltpu.SemaphoreType.DMA((3,)),
            pltpu.SemaphoreType.DMA((3,)),
            pltpu.SemaphoreType.DMA((2 * REACH + 1, ndisp)),
            pltpu.SemaphoreType.DMA((2 * REACH + 1, ndisp)),
        ],
        compiler_params=pltpu.CompilerParams(
            collective_id=0, has_side_effects=True, vmem_limit_bytes=40 * 1024 * 1024
        ),
    )(*[pltpu.with_memory_space_constraint(arg, pltpu.HBM) for arg in args])


def solution(mesh):
    placed = (
        P(("grp", "pix"), None),
        P(("grp", "pix"), None),
        P(),
        P(),
        P(),
        P(),
        P(),
        P(),
        P(),
        P(("grp", "pix"), None),
    )
    return jax.shard_map(
        local,
        mesh=mesh,
        in_specs=placed,
        out_specs=(P(("grp", "pix"), None), P(("grp", "pix"), None)),
        check_vma=False,
    )
```

```python
import functools

import jax
import jax.numpy as jnp
from jax import lax
from jax.experimental import pallas as pl
from jax.experimental.pallas import tpu as pltpu
from jax.sharding import PartitionSpec as P

DSP = 128
UP = 4
TV_ITERS = 8
REACH = 2

dual_step = 0.175
primal_step = 0.7
tv_bound = 0.3
cost_scale = 8.0
mask_scale = 3.0
highest_prec = lax.Precision.HIGHEST
f32 = jnp.float32
bf16 = jnp.bfloat16
LANES = 128
CHUNK1 = 11
CHUNK2 = 8


def iota(shape, dim):
    return lax.broadcasted_iota(jnp.int32, shape, dim)


def one_hot(cond):
    return jnp.where(cond, 1.0, 0.0)


def dot(a, b, dims=((1,), (0,)), precision=None):
    return lax.dot_general(a, b, (dims, ((), ())), precision=precision, preferred_element_type=f32)


def column(row, groups):
    ch = row.shape[1]
    shape = (groups * ch, ch)
    return jnp.sum(
        jnp.where(iota(shape, 0) % ch == iota(shape, 1), jnp.broadcast_to(row, shape), 0.0),
        axis=1,
        keepdims=True,
    )


def split(value):
    high = value.astype(bf16)
    return high, (value - high.astype(f32)).astype(bf16)


def kernel(
    npix, ndisp,
    left_hbm, right_hbm, featw_hbm, w1_hbm, b1_hbm, w2_hbm, b2_hbm, head_hbm, mask_hbm, conf_hbm,
    coarse_ref, out_ref,
    left_ref, right_ref, featw_ref, w1_ref, b1_ref, w2_ref, b2_ref, head_ref, mask_ref, conf_ref,
    load_sem,
    keep_buf, rows_buf, part_buf, wt_buf, wmat_buf, col_buf, lr_buf, hid_buf, score_buf, mix_buf, big_buf,
    rows_send, rows_recv, part_send, part_recv,
):
    fine_rows, fine_cols = left_ref.shape
    rows = fine_rows // UP
    cols = fine_cols // UP
    ch = featw_ref.shape[1]
    planes = DSP // ndisp
    pix = lax.axis_index("pix")
    disp = lax.axis_index("disp")
    start = disp * planes

    def target(k, dc):
        return {"pix": pix + k, "disp": lax.rem(disp + dc, ndisp)}

    def exists(k):
        return (pix + k >= 0) & (pix + k < npix)

    loads = [
        pltpu.make_async_copy(src, dst, load_sem.at[n])
        for n, (src, dst) in enumerate(
            (
                (left_hbm, left_ref),
                (right_hbm, right_ref),
                (conf_hbm, conf_ref),
                (featw_hbm, featw_ref),
                (w1_hbm, w1_ref),
                (w2_hbm, w2_ref),
                (b1_hbm, b1_ref),
                (b2_hbm, b2_ref),
                (head_hbm, head_ref),
                (mask_hbm, mask_ref),
            )
        )
    ]
    for load in loads:
        load.start()

    offsets = [k for k in range(-REACH, REACH + 1)]
    barrier = pltpu.get_barrier_semaphore()
    expected = jnp.int32(0)
    for k in offsets:
        for dc in range(ndisp):
            if k == 0 and dc == 0:
                continue

            @pl.when(exists(k))
            def _():
                pl.semaphore_signal(
                    barrier, inc=1, device_id=target(k, dc), device_id_type=pl.DeviceIdType.MESH
                )

            expected = expected + jnp.where(exists(k), 1, 0)

    block = UP * (cols // UP)
    wide = block // UP
    ii, oo = iota((block, block), 0), iota((block, block), 1)
    undo = one_hot((ii % UP == oo // wide) & (ii // UP == oo % wide)).astype(bf16)
    for load in loads[:4]:
        load.wait()
    stacked = jnp.concatenate(
        [
            (left_ref[...] - 128).astype(f32) / 64.0,
            (right_ref[...] - 128).astype(f32) / 64.0,
            conf_ref[...],
            jnp.zeros((fine_rows, fine_cols), f32),
        ],
        axis=0,
    ).astype(bf16)
    tall = stacked.shape[0]
    blocks = fine_cols // block
    res = dot(
        jnp.concatenate([stacked[:, j * block : (j + 1) * block] for j in range(blocks)], axis=0),
        undo,
    )
    by_b = [
        jnp.concatenate(
            [res[j * tall : (j + 1) * tall, b * wide : (b + 1) * wide] for j in range(blocks)],
            axis=1,
        )
        for b in range(UP)
    ]
    patch_left, patch_right, conf_rows = [
        jnp.concatenate([v[n * fine_rows : (n + 1) * fine_rows] for v in by_b], axis=0)
        for n in range(3)
    ]
    patch_rows = UP * fine_rows
    pp, qq = iota((UP * UP, patch_rows), 0), iota((UP * UP, patch_rows), 1)
    pick = one_hot(pp == UP * (qq % UP) + qq // fine_rows)
    spread = dot(featw_ref[...], pick, ((0,), (0,)), highest_prec)
    spread = jnp.concatenate([spread] * rows, axis=0)
    rr, qq = iota(spread.shape, 0), iota(spread.shape, 1)
    spread = jnp.where(rr // ch == (qq % fine_rows) // UP, spread, 0.0)
    frows = rows * ch
    rows_buf[1, 0:frows, :] = dot(spread, patch_left, precision=highest_prec).astype(bf16)
    rows_buf[1, frows : 2 * frows, :] = dot(spread, patch_right, precision=highest_prec).astype(bf16)
    rows_buf[1, 2 * frows : 2 * frows + patch_rows, :] = conf_rows.astype(bf16)

    pl.semaphore_wait(barrier, expected)

    def rows_copy(k):
        return pltpu.make_async_remote_copy(
            src_ref=rows_buf.at[1],
            dst_ref=rows_buf.at[1 - k],
            send_sem=rows_send.at[1 + k],
            recv_sem=rows_recv.at[1 - k],
            device_id=target(k, 0),
            device_id_type=pl.DeviceIdType.MESH,
        )

    for k in (-1, 1):

        @pl.when(exists(k))
        def _():
            rows_copy(k).start()

        @pl.when(jnp.logical_not(exists(k)))
        def _():
            rows_buf[1 + k] = jnp.zeros(rows_buf.shape[1:], bf16)

    for load in loads[4:]:
        load.wait()

    to, fr = iota((12 * ch, 12 * ch), 0), iota((12 * ch, 12 * ch), 1)
    order = one_hot(fr == (to % 24 // 8) * 4 * ch + to // 24 * 8 + to % 8).astype(bf16)
    for n, w_ref in enumerate((w1_ref, w2_ref)):
        wt_buf[...] = jnp.zeros_like(wt_buf)
        for kd in range(3):
            for ky in range(3):
                for kx in range(3):
                    tap = w_ref[kd, ky, kx].astype(f32)
                    for pd in range(2):
                        for py in range(2):
                            row = ((kd + pd) * 4 + ky + py) * ch
                            col = (kx * 4 + pd * 2 + py) * ch
                            wt_buf[row : row + ch, col : col + ch] = tap
        by_tap = wt_buf[...].T[: 12 * ch].astype(bf16)
        wmat_buf[n] = dot(order, by_tap).astype(bf16)
    group = 4 * ch
    for n, ref in enumerate((b1_ref, b2_ref, head_ref)):
        col_buf[n] = jnp.broadcast_to(column(ref[...], 4), (group, cols))

    deep = 8
    taps = mask_ref.shape[1]
    cc, qq = iota((ch, deep * ch), 0), iota((ch, deep * ch), 1)
    tiled = dot(mask_ref[...], one_hot(cc == qq % ch), ((0,), (0,)), highest_prec)
    shape = (taps, deep, deep * ch)
    big = jnp.where(
        iota(shape, 1) == iota(shape, 2) // ch, jnp.broadcast_to(tiled[:, None, :], shape), 0.0
    ).reshape(taps * deep, deep * ch)
    big_buf[...] = jnp.concatenate(split(big), axis=1)

    step1 = 2 * CHUNK1
    for n in range(1, step1 + 1):
        keep_buf[n] = one_hot(iota(keep_buf.shape[1:], 1) >= n).astype(bf16)

    def rows_wait(k):
        return pltpu.make_async_remote_copy(
            src_ref=rows_buf.at[1],
            dst_ref=rows_buf.at[1 + k],
            send_sem=rows_send.at[1 + k],
            recv_sem=rows_recv.at[1 + k],
            device_id=target(k, 0),
            device_id_type=pl.DeviceIdType.MESH,
        )

    for k in (-1, 1):

        @pl.when(exists(k))
        def _():
            rows_wait(k).wait_recv()

    for slot in range(3):
        for side in range(2):
            lr_buf[side, slot * frows : (slot + 1) * frows, :] = rows_buf[
                slot, side * frows : (side + 1) * frows, :
            ].astype(f32)

    lane = iota((group, LANES), 1)
    not_first = lane >= 1
    not_last = lane < LANES - 1

    def conv(weights, values):
        acc = dot(weights, values).reshape(group // 8, 3, 8, cols)
        tap = [acc[:, kx].reshape(group, cols) for kx in range(3)]
        moved_right, moved_left = {}, {}
        parts = []
        for n in range(cols // LANES):
            at = slice(n * LANES, (n + 1) * LANES)
            moved_right[n] = pltpu.roll(tap[0][:, at], 1, 1)
            moved_left[n] = pltpu.roll(tap[2][:, at], LANES - 1, 1)
        for n in range(cols // LANES):
            at = slice(n * LANES, (n + 1) * LANES)
            before = jnp.where(not_first, moved_right[n], moved_right.get(n - 1, 0.0))
            after = jnp.where(not_last, moved_left[n], moved_left.get(n + 1, 0.0))
            parts.append(tap[1][:, at] + before + after)
        return jnp.concatenate(parts, axis=1)

    def volume(plane):
        shift = lax.rem(plane + cols, cols)
        moved = pltpu.roll(lr_buf[1], shift, 1)
        keep = (iota(moved.shape, 1) >= plane) & (plane >= 0) & (plane < DSP)
        return jnp.where(keep, moved * lr_buf[0], 0.0).astype(bf16)

    vrows = 4 * ch
    half = 2 * ch

    left_rows = lr_buf[0].astype(bf16)
    def shifted(value, n, inside=None):
        if n == 0:
            return value if inside is None else value * inside
        keep = keep_buf[n] if inside is None else keep_buf[n] * inside
        rolled = pltpu.roll(value, n, 1)
        return (rolled.reshape(-1, ch, cols) * keep[None]).reshape(rolled.shape)

    def first(c, carry):
        base = c * step1
        held, origin = list(carry[:2]), carry[2]
        for j in range(CHUNK1):
            held = held[-2:]
            for n in (2 * j, 2 * j + 1):
                inside = None
                if n >= step1 - 2:
                    inside = (start + base + n < DSP).astype(f32).astype(bf16)
                held.append(shifted(origin, n, inside) * left_rows)
            for rb in range(2):
                values = jnp.concatenate([v[rb * half : rb * half + vrows] for v in held], axis=0)
                got = jnp.maximum(conv(wmat_buf[0], values) + col_buf[0], 0.0).astype(bf16)
                for pd in range(2):
                    hid_buf[base + 2 * j + pd, rb * half : (rb + 1) * half, :] = got[
                        pd * half : (pd + 1) * half
                    ]
        return (held[-2], held[-1], shifted(origin, step1))

    opening = jnp.where(
        iota(lr_buf.shape[1:], 1) >= start, pltpu.roll(lr_buf[1], start, 1), 0.0
    ).astype(bf16)
    lax.fori_loop(
        0,
        (planes // 2 + 1) // CHUNK1,
        first,
        (volume(start - 2), volume(start - 1), opening),
    )

    @pl.when(pix == 0)
    def _():
        hid_buf[:, 0:ch, :] = jnp.zeros((planes + 2, ch, cols), bf16)

    @pl.when(pix == npix - 1)
    def _():
        hid_buf[:, 3 * ch : 4 * ch, :] = jnp.zeros((planes + 2, ch, cols), bf16)

    @pl.when(disp == 0)
    def _():
        hid_buf[0] = jnp.zeros((4 * ch, cols), bf16)

    @pl.when(disp == ndisp - 1)
    def _():
        hid_buf[planes + 1] = jnp.zeros((4 * ch, cols), bf16)

    def second(c, carry):
        base = c * CHUNK2
        for j in range(CHUNK2):
            values = hid_buf[pl.ds(2 * (base + j), 4)].reshape(4 * vrows, cols)
            got = jnp.maximum(conv(wmat_buf[1], values) + col_buf[1], 0.0) * col_buf[2]
            score_buf[base + j] = jnp.sum(got.reshape(4, ch, cols), axis=1)
        return carry

    lax.fori_loop(0, planes // 2 // CHUNK2, second, 0)

    expo = jnp.exp(-cost_scale * jnp.tanh(score_buf[...]))
    shape = expo.shape
    plane = start + 2 * iota(shape, 0) + iota(shape, 1) // rows
    weight4 = jnp.sum(expo, axis=0)
    plane4 = jnp.sum(expo * (plane.astype(f32) / DSP), axis=0)
    mine = jnp.concatenate(
        [plane4[0:rows] + plane4[rows:], weight4[0:rows] + weight4[rows:], jnp.ones((4, cols), f32)],
        axis=0,
    )
    part_buf[REACH, disp] = mine

    def part_copy(k, dc):
        return pltpu.make_async_remote_copy(
            src_ref=part_buf.at[REACH, disp],
            dst_ref=part_buf.at[REACH - k, disp],
            send_sem=part_send.at[REACH + k, dc],
            recv_sem=part_recv.at[REACH - k, disp],
            device_id=target(k, dc),
            device_id_type=pl.DeviceIdType.MESH,
        )

    def part_wait(k, dc):
        core = lax.rem(disp + dc, ndisp)
        return pltpu.make_async_remote_copy(
            src_ref=part_buf.at[REACH, disp],
            dst_ref=part_buf.at[REACH + k, core],
            send_sem=part_send.at[REACH + k, dc],
            recv_sem=part_recv.at[REACH + k, core],
            device_id=target(k, dc),
            device_id_type=pl.DeviceIdType.MESH,
        )

    partners = [(k, dc) for k in (2, -2, 1, -1, 0) for dc in range(ndisp) if (k, dc) != (0, 0)]
    for k, dc in partners:

        @pl.when(exists(k))
        def _():
            part_copy(k, dc).start()

    for k in (-2, -1, 1, 2):

        @pl.when(jnp.logical_not(exists(k)))
        def _():
            for core in range(ndisp):
                part_buf[REACH + k, core] = jnp.where(iota((8, cols), 0) < rows, 0.0, 1.0)

    none = jnp.zeros((ch, cols), bf16)
    lines = jnp.concatenate(
        [none] + [rows_buf[slot, 0:frows, :] for slot in range(3)] + [none], axis=0
    )
    logits = dot(big_buf[...], jnp.concatenate([lines, lines], axis=0))
    expo = jnp.exp(mask_scale * jnp.tanh(logits)).reshape(9, UP * UP, deep, cols)
    mix_buf[...] = expo * (1.0 / jnp.sum(expo, axis=0))[None]

    conf_all = jnp.concatenate(
        [rows_buf[slot, 2 * frows : 2 * frows + patch_rows, :] for slot in range(3)], axis=0
    )
    shape = (UP * UP * deep, 3 * patch_rows)
    to, fr = iota(shape, 0), iota(shape, 1)
    to_a, to_b, to_s = to // (UP * deep), (to // deep) % UP, to % deep
    fr_slot, fr_b, fr_r, fr_a = fr // patch_rows, (fr // fine_rows) % UP, (fr // UP) % rows, fr % UP
    place = one_hot((to_a == fr_a) & (to_b == fr_b) & (to_s - 1 == fr_slot * rows + fr_r))
    fidelity = dot(place.astype(bf16), conf_all).reshape(UP, UP, deep, cols)
    inverse = 1.0 / (1.0 + primal_step * fidelity)

    for k, dc in partners:

        @pl.when(exists(k))
        def _():
            part_wait(k, dc).wait_recv()

    total = part_buf[:, 0]
    for core in range(1, ndisp):
        total = total + part_buf[:, core]
    ratio = [total[n][0:rows] / total[n][rows : 2 * rows] for n in range(2 * REACH + 1)]
    coarse_ref[...] = ratio[REACH]
    coarse = jnp.concatenate([ratio[0][1:2]] + ratio[1:-1] + [ratio[-1][0:1]], axis=0)

    lane8 = iota((deep, cols), 1)
    lane_first, lane_last = lane8 >= 1, lane8 < cols - 1
    initial = None
    for ky in range(3):
        line = coarse if ky == 1 else pltpu.roll(coarse, (1 - ky) % deep, 0)
        for kx in range(3):
            if kx == 0:
                near = jnp.where(lane_first, pltpu.roll(line, 1, 1), 0.0)
            elif kx == 2:
                near = jnp.where(lane_last, pltpu.roll(line, cols - 1, 1), 0.0)
            else:
                near = line
            term = mix_buf[3 * ky + kx] * near[None]
            initial = term if initial is None else initial + term
    initial = initial.reshape(UP, UP, deep, cols)
    pull = primal_step * inverse
    constant = pull * fidelity * initial

    line = pix * rows - 3 + iota((deep, cols), 0)
    inside_last = (line >= 0) & (line < npix * rows - 1)

    def tv(step, current):
        primal, extrap, dual_x, dual_y = current
        over = [
            jnp.where(lane_last, pltpu.roll(extrap[a, 0], cols - 1, 1) - extrap[a, UP - 1], 0.0)
            for a in range(UP)
        ]
        grad_x = jnp.concatenate(
            [extrap[:, 1:] - extrap[:, :-1], jnp.stack(over)[:, None]], axis=1
        )
        under = [
            jnp.where(inside_last, pltpu.roll(extrap[0, b], deep - 1, 0) - extrap[UP - 1, b], 0.0)
            for b in range(UP)
        ]
        grad_y = jnp.concatenate(
            [extrap[1:] - extrap[:-1], jnp.stack(under)[None]], axis=0
        )
        trial_x = dual_x + grad_x
        trial_y = dual_y + grad_y
        square = jnp.maximum(trial_x * trial_x + trial_y * trial_y, 1e-30)
        shrink = jnp.minimum(1.0, tv_bound * lax.rsqrt(square))
        dual_x = trial_x * shrink
        dual_y = trial_y * shrink
        prior = [
            jnp.where(lane_first, pltpu.roll(dual_x[a, UP - 1], 1, 1), 0.0) for a in range(UP)
        ]
        left = jnp.concatenate([jnp.stack(prior)[:, None], dual_x[:, :-1]], axis=1)
        above = [pltpu.roll(dual_y[UP - 1, b], 1, 0) for b in range(UP)]
        upper = jnp.concatenate([jnp.stack(above)[None], dual_y[:-1]], axis=0)
        divergence = dual_x - left + dual_y - upper
        updated = primal * inverse + divergence * pull + constant
        return (updated, (2.0 * dual_step) * updated - dual_step * primal, dual_x, dual_y)

    zeros = jnp.zeros_like(initial)
    result = lax.fori_loop(
        0, TV_ITERS, tv, (initial, dual_step * initial, zeros, zeros), unroll=4
    )[0]

    shape = (fine_rows, UP * deep)
    to, fr = iota(shape, 0), iota(shape, 1)
    own = one_hot((to % UP == fr // deep) & (to // UP + 3 == fr % deep)).astype(bf16)
    pieces = []
    for b in range(UP):
        high, low = split(result[:, b].reshape(UP * deep, cols))
        pieces.append(jnp.concatenate([dot(own, high), dot(own, low)], axis=0).astype(bf16))
    redo = one_hot((oo % UP == ii // wide) & (oo // UP == ii % wide)).astype(bf16)
    for j in range(blocks):
        packed = jnp.concatenate([v[:, j * wide : (j + 1) * wide] for v in pieces], axis=1)
        both = dot(packed, redo)
        out_ref[:, j * block : (j + 1) * block] = both[0:fine_rows] + both[fine_rows:]

    for k in (-1, 1):

        @pl.when(exists(k))
        def _():
            rows_copy(k).wait_send()

    for k, dc in partners:

        @pl.when(exists(k))
        def _():
            part_copy(k, dc).wait_send()


def local(
    left_image, right_image, feat_weight, first_weight, first_bias,
    second_weight, second_bias, head_weight, mask_weight, confidence,
):
    npix, ndisp = lax.axis_size("pix"), lax.axis_size("disp")
    fine_rows, fine_cols = left_image.shape
    rows, cols = fine_rows // UP, fine_cols // UP
    ch = feat_weight.shape[1]
    planes = DSP // ndisp
    assert fine_rows == TV_ITERS and rows == 2
    vmem = pl.BlockSpec(memory_space=pltpu.VMEM)
    args = (
        left_image, right_image, feat_weight, first_weight, first_bias[None],
        second_weight, second_bias[None], head_weight[None], mask_weight, confidence,
    )
    return pl.pallas_call(
        functools.partial(kernel, npix, ndisp),
        out_shape=(
            jax.ShapeDtypeStruct((rows, cols), f32),
            jax.ShapeDtypeStruct((fine_rows, fine_cols), f32),
        ),
        in_specs=[pl.BlockSpec(memory_space=pltpu.HBM)] * 10,
        out_specs=(vmem, vmem),
        scratch_shapes=[pltpu.VMEM(arg.shape, arg.dtype) for arg in args]
        + [
            pltpu.SemaphoreType.DMA((len(args),)),
            pltpu.VMEM((2 * CHUNK1 + 1, ch, cols), bf16),
            pltpu.VMEM((3, 2 * rows * ch + UP * fine_rows, cols), bf16),
            pltpu.VMEM((2 * REACH + 1, ndisp, 8, cols), f32),
            pltpu.VMEM((16 * ch, 16 * ch), f32),
            pltpu.VMEM((2, 12 * ch, 16 * ch), bf16),
            pltpu.VMEM((3, 4 * ch, cols), f32),
            pltpu.VMEM((2, 3 * rows * ch, cols), f32),
            pltpu.VMEM((planes + 2, 4 * ch, cols), bf16),
            pltpu.VMEM((planes // 2, 2 * rows, cols), f32),
            pltpu.VMEM((9, UP * UP, 8, cols), f32),
            pltpu.VMEM((mask_weight.shape[1] * 8, 2 * 8 * ch), bf16),
            pltpu.SemaphoreType.DMA((3,)),
            pltpu.SemaphoreType.DMA((3,)),
            pltpu.SemaphoreType.DMA((2 * REACH + 1, ndisp)),
            pltpu.SemaphoreType.DMA((2 * REACH + 1, ndisp)),
        ],
        compiler_params=pltpu.CompilerParams(
            collective_id=0, has_side_effects=True, vmem_limit_bytes=40 * 1024 * 1024
        ),
    )(*[pltpu.with_memory_space_constraint(arg, pltpu.HBM) for arg in args])


def solution(mesh):
    placed = (
        P(("grp", "pix"), None),
        P(("grp", "pix"), None),
        P(),
        P(),
        P(),
        P(),
        P(),
        P(),
        P(),
        P(("grp", "pix"), None),
    )
    return jax.shard_map(
        local,
        mesh=mesh,
        in_specs=placed,
        out_specs=(P(("grp", "pix"), None), P(("grp", "pix"), None)),
        check_vma=False,
    )
```

```python
import functools

import jax
import jax.numpy as jnp
from jax import lax
from jax.experimental import pallas as pl
from jax.experimental.pallas import tpu as pltpu
from jax.sharding import PartitionSpec as P

DSP = 128
UP = 4
TV_ITERS = 8
REACH = 2

dual_step = 0.175
primal_step = 0.7
tv_bound = 0.3
cost_scale = 8.0
mask_scale = 3.0
highest_prec = lax.Precision.HIGHEST
f32 = jnp.float32
bf16 = jnp.bfloat16
LANES = 128
CHUNK1 = 11
CHUNK2 = 8


def iota(shape, dim):
    return lax.broadcasted_iota(jnp.int32, shape, dim)


def one_hot(cond):
    return jnp.where(cond, 1.0, 0.0)


def dot(a, b, dims=((1,), (0,)), precision=None):
    return lax.dot_general(a, b, (dims, ((), ())), precision=precision, preferred_element_type=f32)


def column(row, groups):
    ch = row.shape[1]
    shape = (groups * ch, ch)
    return jnp.sum(
        jnp.where(iota(shape, 0) % ch == iota(shape, 1), jnp.broadcast_to(row, shape), 0.0),
        axis=1,
        keepdims=True,
    )


def split(value):
    high = value.astype(bf16)
    return high, (value - high.astype(f32)).astype(bf16)


def kernel(
    npix, ndisp,
    left_hbm, right_hbm, featw_hbm, w1_hbm, b1_hbm, w2_hbm, b2_hbm, head_hbm, mask_hbm, conf_hbm,
    coarse_ref, out_ref,
    left_ref, right_ref, featw_ref, w1_ref, b1_ref, w2_ref, b2_ref, head_ref, mask_ref, conf_ref,
    load_sem,
    keep_buf, rows_buf, part_buf, wt_buf, wmat_buf, col_buf, lr_buf, hid_buf, score_buf, mix_buf, big_buf,
    rows_send, rows_recv, part_send, part_recv,
):
    fine_rows, fine_cols = left_ref.shape
    rows = fine_rows // UP
    cols = fine_cols // UP
    ch = featw_ref.shape[1]
    planes = DSP // ndisp
    pix = lax.axis_index("pix")
    disp = lax.axis_index("disp")
    start = disp * planes

    def target(k, dc):
        return {"pix": pix + k, "disp": lax.rem(disp + dc, ndisp)}

    def exists(k):
        return (pix + k >= 0) & (pix + k < npix)

    loads = [
        pltpu.make_async_copy(src, dst, load_sem.at[n])
        for n, (src, dst) in enumerate(
            (
                (left_hbm, left_ref),
                (right_hbm, right_ref),
                (conf_hbm, conf_ref),
                (featw_hbm, featw_ref),
                (w1_hbm, w1_ref),
                (w2_hbm, w2_ref),
                (b1_hbm, b1_ref),
                (b2_hbm, b2_ref),
                (head_hbm, head_ref),
                (mask_hbm, mask_ref),
            )
        )
    ]
    for load in loads:
        load.start()

    offsets = [k for k in range(-REACH, REACH + 1)]
    barrier = pltpu.get_barrier_semaphore()
    expected = jnp.int32(0)
    for k in offsets:
        for dc in range(ndisp):
            if k == 0 and dc == 0:
                continue

            @pl.when(exists(k))
            def _():
                pl.semaphore_signal(
                    barrier, inc=1, device_id=target(k, dc), device_id_type=pl.DeviceIdType.MESH
                )

            expected = expected + jnp.where(exists(k), 1, 0)

    block = UP * (cols // UP)
    wide = block // UP
    ii, oo = iota((block, block), 0), iota((block, block), 1)
    undo = one_hot((ii % UP == oo // wide) & (ii // UP == oo % wide)).astype(bf16)
    for load in loads[:4]:
        load.wait()
    stacked = jnp.concatenate(
        [
            (left_ref[...] - 128).astype(f32) / 64.0,
            (right_ref[...] - 128).astype(f32) / 64.0,
            conf_ref[...],
            jnp.zeros((fine_rows, fine_cols), f32),
        ],
        axis=0,
    ).astype(bf16)
    tall = stacked.shape[0]
    blocks = fine_cols // block
    res = dot(
        jnp.concatenate([stacked[:, j * block : (j + 1) * block] for j in range(blocks)], axis=0),
        undo,
    )
    by_b = [
        jnp.concatenate(
            [res[j * tall : (j + 1) * tall, b * wide : (b + 1) * wide] for j in range(blocks)],
            axis=1,
        )
        for b in range(UP)
    ]
    patch_left, patch_right, conf_rows = [
        jnp.concatenate([v[n * fine_rows : (n + 1) * fine_rows] for v in by_b], axis=0)
        for n in range(3)
    ]
    patch_rows = UP * fine_rows
    pp, qq = iota((UP * UP, patch_rows), 0), iota((UP * UP, patch_rows), 1)
    pick = one_hot(pp == UP * (qq % UP) + qq // fine_rows)
    spread = dot(featw_ref[...], pick, ((0,), (0,)), highest_prec)
    spread = jnp.concatenate([spread] * rows, axis=0)
    rr, qq = iota(spread.shape, 0), iota(spread.shape, 1)
    spread = jnp.where(rr // ch == (qq % fine_rows) // UP, spread, 0.0)
    frows = rows * ch
    rows_buf[1, 0:frows, :] = dot(spread, patch_left, precision=highest_prec).astype(bf16)
    rows_buf[1, frows : 2 * frows, :] = dot(spread, patch_right, precision=highest_prec).astype(bf16)
    rows_buf[1, 2 * frows : 2 * frows + patch_rows, :] = conf_rows.astype(bf16)

    pl.semaphore_wait(barrier, expected)

    def rows_copy(k):
        return pltpu.make_async_remote_copy(
            src_ref=rows_buf.at[1],
            dst_ref=rows_buf.at[1 - k],
            send_sem=rows_send.at[1 + k],
            recv_sem=rows_recv.at[1 - k],
            device_id=target(k, 0),
            device_id_type=pl.DeviceIdType.MESH,
        )

    for k in (-1, 1):

        @pl.when(exists(k))
        def _():
            rows_copy(k).start()

        @pl.when(jnp.logical_not(exists(k)))
        def _():
            rows_buf[1 + k] = jnp.zeros(rows_buf.shape[1:], bf16)

    for load in loads[4:]:
        load.wait()

    to, fr = iota((12 * ch, 12 * ch), 0), iota((12 * ch, 12 * ch), 1)
    order = one_hot(fr == (to % 24 // 8) * 4 * ch + to // 24 * 8 + to % 8).astype(bf16)
    for n, w_ref in enumerate((w1_ref, w2_ref)):
        wt_buf[...] = jnp.zeros_like(wt_buf)
        for kd in range(3):
            for ky in range(3):
                for kx in range(3):
                    tap = w_ref[kd, ky, kx].astype(f32)
                    for pd in range(2):
                        for py in range(2):
                            row = ((kd + pd) * 4 + ky + py) * ch
                            col = (kx * 4 + pd * 2 + py) * ch
                            wt_buf[row : row + ch, col : col + ch] = tap
        by_tap = wt_buf[...].T[: 12 * ch].astype(bf16)
        wmat_buf[n] = dot(order, by_tap).astype(bf16)
    group = 4 * ch
    for n, ref in enumerate((b1_ref, b2_ref, head_ref)):
        col_buf[n] = jnp.broadcast_to(column(ref[...], 4), (group, cols))

    deep = 8
    taps = mask_ref.shape[1]
    cc, qq = iota((ch, deep * ch), 0), iota((ch, deep * ch), 1)
    tiled = dot(mask_ref[...], one_hot(cc == qq % ch), ((0,), (0,)), highest_prec)
    shape = (taps, deep, deep * ch)
    big = jnp.where(
        iota(shape, 1) == iota(shape, 2) // ch, jnp.broadcast_to(tiled[:, None, :], shape), 0.0
    ).reshape(taps * deep, deep * ch)
    big_buf[...] = jnp.concatenate(split(big), axis=1)

    step1 = 2 * CHUNK1
    for n in range(1, step1 + 1):
        keep_buf[n] = one_hot(iota(keep_buf.shape[1:], 1) >= n).astype(bf16)

    def rows_wait(k):
        return pltpu.make_async_remote_copy(
            src_ref=rows_buf.at[1],
            dst_ref=rows_buf.at[1 + k],
            send_sem=rows_send.at[1 + k],
            recv_sem=rows_recv.at[1 + k],
            device_id=target(k, 0),
            device_id_type=pl.DeviceIdType.MESH,
        )

    for k in (-1, 1):

        @pl.when(exists(k))
        def _():
            rows_wait(k).wait_recv()

    for slot in range(3):
        for side in range(2):
            lr_buf[side, slot * frows : (slot + 1) * frows, :] = rows_buf[
                slot, side * frows : (side + 1) * frows, :
            ].astype(f32)

    lane = iota((group, LANES), 1)
    not_first = lane >= 1
    not_last = lane < LANES - 1

    def finish(acc):
        acc = acc.reshape(group // 8, 3, 8, cols)
        tap = [acc[:, kx].reshape(group, cols) for kx in range(3)]
        moved_right, moved_left = {}, {}
        parts = []
        for n in range(cols // LANES):
            at = slice(n * LANES, (n + 1) * LANES)
            moved_right[n] = pltpu.roll(tap[0][:, at], 1, 1)
            moved_left[n] = pltpu.roll(tap[2][:, at], LANES - 1, 1)
        for n in range(cols // LANES):
            at = slice(n * LANES, (n + 1) * LANES)
            before = jnp.where(not_first, moved_right[n], moved_right.get(n - 1, 0.0))
            after = jnp.where(not_last, moved_left[n], moved_left.get(n + 1, 0.0))
            parts.append(tap[1][:, at] + before + after)
        return jnp.concatenate(parts, axis=1)

    def volume(plane):
        shift = lax.rem(plane + cols, cols)
        moved = pltpu.roll(lr_buf[1], shift, 1)
        keep = (iota(moved.shape, 1) >= plane) & (plane >= 0) & (plane < DSP)
        return jnp.where(keep, moved * lr_buf[0], 0.0).astype(bf16)

    vrows = 4 * ch
    half = 2 * ch

    left_rows = lr_buf[0].astype(bf16)
    def shifted(value, n, inside=None):
        if n == 0:
            return value if inside is None else value * inside
        keep = keep_buf[n] if inside is None else keep_buf[n] * inside
        rolled = pltpu.roll(value, n, 1)
        return (rolled.reshape(-1, ch, cols) * keep[None]).reshape(rolled.shape)

    def first(c, carry):
        base = c * step1
        held, origin = list(carry[:2]), carry[2]
        waiting = None

        def close(pending):
            j, accs = pending
            for rb in range(2):
                got = jnp.maximum(finish(accs[rb]) + col_buf[0], 0.0).astype(bf16)
                for pd in range(2):
                    hid_buf[base + 2 * j + pd, rb * half : (rb + 1) * half, :] = got[
                        pd * half : (pd + 1) * half
                    ]

        for j in range(CHUNK1):
            held = held[-2:]
            for n in (2 * j, 2 * j + 1):
                inside = None
                if n >= step1 - 2:
                    inside = (start + base + n < DSP).astype(f32).astype(bf16)
                held.append(shifted(origin, n, inside) * left_rows)
            accs = []
            for rb in range(2):
                values = jnp.concatenate([v[rb * half : rb * half + vrows] for v in held], axis=0)
                accs.append(dot(wmat_buf[0], values))
            if waiting is not None:
                close(waiting)
            waiting = (j, accs)
        close(waiting)
        return (held[-2], held[-1], shifted(origin, step1))

    opening = jnp.where(
        iota(lr_buf.shape[1:], 1) >= start, pltpu.roll(lr_buf[1], start, 1), 0.0
    ).astype(bf16)
    lax.fori_loop(
        0,
        (planes // 2 + 1) // CHUNK1,
        first,
        (volume(start - 2), volume(start - 1), opening),
    )

    @pl.when(pix == 0)
    def _():
        hid_buf[:, 0:ch, :] = jnp.zeros((planes + 2, ch, cols), bf16)

    @pl.when(pix == npix - 1)
    def _():
        hid_buf[:, 3 * ch : 4 * ch, :] = jnp.zeros((planes + 2, ch, cols), bf16)

    @pl.when(disp == 0)
    def _():
        hid_buf[0] = jnp.zeros((4 * ch, cols), bf16)

    @pl.when(disp == ndisp - 1)
    def _():
        hid_buf[planes + 1] = jnp.zeros((4 * ch, cols), bf16)

    def second(c, carry):
        base = c * CHUNK2
        waiting = None

        def close(pending):
            j, acc = pending
            got = jnp.maximum(finish(acc) + col_buf[1], 0.0) * col_buf[2]
            score_buf[base + j] = jnp.sum(got.reshape(4, ch, cols), axis=1)

        for j in range(CHUNK2):
            values = hid_buf[pl.ds(2 * (base + j), 4)].reshape(4 * vrows, cols)
            acc = dot(wmat_buf[1], values)
            if waiting is not None:
                close(waiting)
            waiting = (j, acc)
        close(waiting)
        return carry

    lax.fori_loop(0, planes // 2 // CHUNK2, second, 0)

    expo = jnp.exp(-cost_scale * jnp.tanh(score_buf[...]))
    shape = expo.shape
    plane = start + 2 * iota(shape, 0) + iota(shape, 1) // rows
    weight4 = jnp.sum(expo, axis=0)
    plane4 = jnp.sum(expo * (plane.astype(f32) / DSP), axis=0)
    mine = jnp.concatenate(
        [plane4[0:rows] + plane4[rows:], weight4[0:rows] + weight4[rows:], jnp.ones((4, cols), f32)],
        axis=0,
    )
    part_buf[REACH, disp] = mine

    def part_copy(k, dc):
        return pltpu.make_async_remote_copy(
            src_ref=part_buf.at[REACH, disp],
            dst_ref=part_buf.at[REACH - k, disp],
            send_sem=part_send.at[REACH + k, dc],
            recv_sem=part_recv.at[REACH - k, disp],
            device_id=target(k, dc),
            device_id_type=pl.DeviceIdType.MESH,
        )

    def part_wait(k, dc):
        core = lax.rem(disp + dc, ndisp)
        return pltpu.make_async_remote_copy(
            src_ref=part_buf.at[REACH, disp],
            dst_ref=part_buf.at[REACH + k, core],
            send_sem=part_send.at[REACH + k, dc],
            recv_sem=part_recv.at[REACH + k, core],
            device_id=target(k, dc),
            device_id_type=pl.DeviceIdType.MESH,
        )

    partners = [(k, dc) for k in (2, -2, 1, -1, 0) for dc in range(ndisp) if (k, dc) != (0, 0)]
    for k, dc in partners:

        @pl.when(exists(k))
        def _():
            part_copy(k, dc).start()

    for k in (-2, -1, 1, 2):

        @pl.when(jnp.logical_not(exists(k)))
        def _():
            for core in range(ndisp):
                part_buf[REACH + k, core] = jnp.where(iota((8, cols), 0) < rows, 0.0, 1.0)

    none = jnp.zeros((ch, cols), bf16)
    lines = jnp.concatenate(
        [none] + [rows_buf[slot, 0:frows, :] for slot in range(3)] + [none], axis=0
    )
    logits = dot(big_buf[...], jnp.concatenate([lines, lines], axis=0))
    expo = jnp.exp(mask_scale * jnp.tanh(logits)).reshape(9, UP * UP, deep, cols)
    mix_buf[...] = expo * (1.0 / jnp.sum(expo, axis=0))[None]

    conf_all = jnp.concatenate(
        [rows_buf[slot, 2 * frows : 2 * frows + patch_rows, :] for slot in range(3)], axis=0
    )
    shape = (UP * UP * deep, 3 * patch_rows)
    to, fr = iota(shape, 0), iota(shape, 1)
    to_a, to_b, to_s = to // (UP * deep), (to // deep) % UP, to % deep
    fr_slot, fr_b, fr_r, fr_a = fr // patch_rows, (fr // fine_rows) % UP, (fr // UP) % rows, fr % UP
    place = one_hot((to_a == fr_a) & (to_b == fr_b) & (to_s - 1 == fr_slot * rows + fr_r))
    fidelity = dot(place.astype(bf16), conf_all).reshape(UP, UP, deep, cols)
    inverse = 1.0 / (1.0 + primal_step * fidelity)

    for k, dc in partners:

        @pl.when(exists(k))
        def _():
            part_wait(k, dc).wait_recv()

    total = part_buf[:, 0]
    for core in range(1, ndisp):
        total = total + part_buf[:, core]
    ratio = [total[n][0:rows] / total[n][rows : 2 * rows] for n in range(2 * REACH + 1)]
    coarse_ref[...] = ratio[REACH]
    coarse = jnp.concatenate([ratio[0][1:2]] + ratio[1:-1] + [ratio[-1][0:1]], axis=0)

    lane8 = iota((deep, cols), 1)
    lane_first, lane_last = lane8 >= 1, lane8 < cols - 1
    initial = None
    for ky in range(3):
        line = coarse if ky == 1 else pltpu.roll(coarse, (1 - ky) % deep, 0)
        for kx in range(3):
            if kx == 0:
                near = jnp.where(lane_first, pltpu.roll(line, 1, 1), 0.0)
            elif kx == 2:
                near = jnp.where(lane_last, pltpu.roll(line, cols - 1, 1), 0.0)
            else:
                near = line
            term = mix_buf[3 * ky + kx] * near[None]
            initial = term if initial is None else initial + term
    initial = initial.reshape(UP, UP, deep, cols)
    pull = primal_step * inverse
    constant = pull * fidelity * initial

    line = pix * rows - 3 + iota((deep, cols), 0)
    inside_last = (line >= 0) & (line < npix * rows - 1)

    def tv(step, current):
        primal, extrap, dual_x, dual_y = current
        over = [
            jnp.where(lane_last, pltpu.roll(extrap[a, 0], cols - 1, 1) - extrap[a, UP - 1], 0.0)
            for a in range(UP)
        ]
        grad_x = jnp.concatenate(
            [extrap[:, 1:] - extrap[:, :-1], jnp.stack(over)[:, None]], axis=1
        )
        under = [
            jnp.where(inside_last, pltpu.roll(extrap[0, b], deep - 1, 0) - extrap[UP - 1, b], 0.0)
            for b in range(UP)
        ]
        grad_y = jnp.concatenate(
            [extrap[1:] - extrap[:-1], jnp.stack(under)[None]], axis=0
        )
        trial_x = dual_x + grad_x
        trial_y = dual_y + grad_y
        square = jnp.maximum(trial_x * trial_x + trial_y * trial_y, 1e-30)
        shrink = jnp.minimum(1.0, tv_bound * lax.rsqrt(square))
        dual_x = trial_x * shrink
        dual_y = trial_y * shrink
        prior = [
            jnp.where(lane_first, pltpu.roll(dual_x[a, UP - 1], 1, 1), 0.0) for a in range(UP)
        ]
        left = jnp.concatenate([jnp.stack(prior)[:, None], dual_x[:, :-1]], axis=1)
        above = [pltpu.roll(dual_y[UP - 1, b], 1, 0) for b in range(UP)]
        upper = jnp.concatenate([jnp.stack(above)[None], dual_y[:-1]], axis=0)
        divergence = dual_x - left + dual_y - upper
        updated = primal * inverse + divergence * pull + constant
        return (updated, (2.0 * dual_step) * updated - dual_step * primal, dual_x, dual_y)

    zeros = jnp.zeros_like(initial)
    result = lax.fori_loop(
        0, TV_ITERS, tv, (initial, dual_step * initial, zeros, zeros), unroll=4
    )[0]

    shape = (fine_rows, UP * deep)
    to, fr = iota(shape, 0), iota(shape, 1)
    own = one_hot((to % UP == fr // deep) & (to // UP + 3 == fr % deep)).astype(bf16)
    pieces = []
    for b in range(UP):
        high, low = split(result[:, b].reshape(UP * deep, cols))
        pieces.append(jnp.concatenate([dot(own, high), dot(own, low)], axis=0).astype(bf16))
    redo = one_hot((oo % UP == ii // wide) & (oo // UP == ii % wide)).astype(bf16)
    for j in range(blocks):
        packed = jnp.concatenate([v[:, j * wide : (j + 1) * wide] for v in pieces], axis=1)
        both = dot(packed, redo)
        out_ref[:, j * block : (j + 1) * block] = both[0:fine_rows] + both[fine_rows:]

    for k in (-1, 1):

        @pl.when(exists(k))
        def _():
            rows_copy(k).wait_send()

    for k, dc in partners:

        @pl.when(exists(k))
        def _():
            part_copy(k, dc).wait_send()


def local(
    left_image, right_image, feat_weight, first_weight, first_bias,
    second_weight, second_bias, head_weight, mask_weight, confidence,
):
    npix, ndisp = lax.axis_size("pix"), lax.axis_size("disp")
    fine_rows, fine_cols = left_image.shape
    rows, cols = fine_rows // UP, fine_cols // UP
    ch = feat_weight.shape[1]
    planes = DSP // ndisp
    assert fine_rows == TV_ITERS and rows == 2
    vmem = pl.BlockSpec(memory_space=pltpu.VMEM)
    args = (
        left_image, right_image, feat_weight, first_weight, first_bias[None],
        second_weight, second_bias[None], head_weight[None], mask_weight, confidence,
    )
    return pl.pallas_call(
        functools.partial(kernel, npix, ndisp),
        out_shape=(
            jax.ShapeDtypeStruct((rows, cols), f32),
            jax.ShapeDtypeStruct((fine_rows, fine_cols), f32),
        ),
        in_specs=[pl.BlockSpec(memory_space=pltpu.HBM)] * 10,
        out_specs=(vmem, vmem),
        scratch_shapes=[pltpu.VMEM(arg.shape, arg.dtype) for arg in args]
        + [
            pltpu.SemaphoreType.DMA((len(args),)),
            pltpu.VMEM((2 * CHUNK1 + 1, ch, cols), bf16),
            pltpu.VMEM((3, 2 * rows * ch + UP * fine_rows, cols), bf16),
            pltpu.VMEM((2 * REACH + 1, ndisp, 8, cols), f32),
            pltpu.VMEM((16 * ch, 16 * ch), f32),
            pltpu.VMEM((2, 12 * ch, 16 * ch), bf16),
            pltpu.VMEM((3, 4 * ch, cols), f32),
            pltpu.VMEM((2, 3 * rows * ch, cols), f32),
            pltpu.VMEM((planes + 2, 4 * ch, cols), bf16),
            pltpu.VMEM((planes // 2, 2 * rows, cols), f32),
            pltpu.VMEM((9, UP * UP, 8, cols), f32),
            pltpu.VMEM((mask_weight.shape[1] * 8, 2 * 8 * ch), bf16),
            pltpu.SemaphoreType.DMA((3,)),
            pltpu.SemaphoreType.DMA((3,)),
            pltpu.SemaphoreType.DMA((2 * REACH + 1, ndisp)),
            pltpu.SemaphoreType.DMA((2 * REACH + 1, ndisp)),
        ],
        compiler_params=pltpu.CompilerParams(
            collective_id=0, has_side_effects=True, vmem_limit_bytes=40 * 1024 * 1024
        ),
    )(*[pltpu.with_memory_space_constraint(arg, pltpu.HBM) for arg in args])


def solution(mesh):
    placed = (
        P(("grp", "pix"), None),
        P(("grp", "pix"), None),
        P(),
        P(),
        P(),
        P(),
        P(),
        P(),
        P(),
        P(("grp", "pix"), None),
    )
    return jax.shard_map(
        local,
        mesh=mesh,
        in_specs=placed,
        out_specs=(P(("grp", "pix"), None), P(("grp", "pix"), None)),
        check_vma=False,
    )
```
